256 devices in a mesh: dp: 32 (over z, x_lo, core), mp: 8 (over x_hi, y).
Axes of the slice: x: 4 (x_hi: 2, x_lo: 2; x = x_hi * 2 + x_lo), y: 4, z: 8, core: 2. Of those that a mesh axis runs over, the one named last changes fastest.
Arguments:
- hidden: bfloat16 [64, 128, 5120], P('dp'), may hold values from -6 to 6
- kv_weight: bfloat16 [2, 5120, 1024], P(None, None, 'mp'), may hold values from -0.078125 to 0.078125
- queries: bfloat16 [64, 128, 8192], P('dp', None, 'mp'), may hold values from -190 to 190
- out_grad: bfloat16 [64, 128, 8192], P('dp', None, 'mp'), may hold values from -6 to 6
- parents: int32 [64], replicated, may hold values from -1 to 38, as said below
- placement: int32 [64], replicated, may hold values from 0 to 63, as said below
- lengths: int32 [64], replicated, may hold values from 16 to 128
Outputs:
- attended: bfloat16 [64, 128, 8192], P('dp', None, 'mp')
- query_grad: bfloat16 [64, 128, 8192], P('dp', None, 'mp')
- hidden_grad: bfloat16 [64, 128, 5120], P('dp', None, 'mp')
- weight_grad: float32 [2, 5120, 1024], P(None, 'dp', 'mp')
The draws below stay inside these ranges and needn't reach their ends.
Inputs may be any that keep to these rules, and one draw needn't show every extreme that they name: `parents`: two trees of 32 segments each, numbered tree by tree; a parent has a smaller number than its child; every root-to-leaf chain has at most 4 segments. `placement`: A permutation of the slots; slot s lies on dp index s // 2; the 2 slots of one dp index hold at most one segment that is the parent of some segment.
All inputs are finite; a program needn't handle non-finite values.
Results may differ from the reference program's by a relative error of at most 0.02.
Values may be sent and summed in bfloat16 or wider, within the bound.
No kernel may reach another device: no remote copies, remote signals or barrier semaphores. Data moves between devices by JAX's collectives and lax.ppermute only.
A program may use at most 128 MiB of HBM per device.

```python
import jax
import jax.numpy as jnp
from jax import lax

D = 5120
QH = 64
KVH = 8
HD = 128
SEG_LEN = 128
DEPTH = 4
SEG_DEV = 2
SLOTS = 64
N_DP = 32


def draw_queries(key, part):
    key = jax.random.fold_in(key, 11)
    key_base = jax.random.fold_in(key, 0)
    shape = (SLOTS, SEG_LEN, QH * HD)
    base = jnp.clip(jax.random.normal(key_base, shape, jnp.float32), -6.0, 6.0)
    return base.astype(jnp.bfloat16)


def draw_parents(key, part):
    key = jax.random.fold_in(key, 5)
    half = SLOTS // 2
    local = jnp.arange(half, dtype=jnp.int32)[None, :]
    chosen = jax.random.randint(key, (2, half), 0, 4).astype(jnp.int32)
    leaf_rank = local - 7
    leaf_parent = 3 + jnp.where(leaf_rank < 4, leaf_rank, chosen)
    inner_parent = jnp.where(local == 0, -1, jnp.where(local < 3, 0, 1 + (local - 3) // 2))
    tree_parent = jnp.where(local < 7, inner_parent, leaf_parent)
    offset = jnp.arange(2, dtype=jnp.int32)[:, None] * half
    return jnp.where(tree_parent >= 0, tree_parent + offset, -1).reshape(SLOTS).astype(jnp.int32)


def draw_placement(key, part):
    key = jax.random.fold_in(key, 7)
    key_device, key_offset, key_rest = jax.random.split(key, 3)
    half = SLOTS // 2
    devices = jax.random.permutation(key_device, N_DP)[:14].astype(jnp.int32)
    offsets = jax.random.randint(key_offset, (14,), 0, SEG_DEV).astype(jnp.int32)
    inner_slots = devices * SEG_DEV + offsets
    taken = jnp.zeros((SLOTS,), jnp.int32).at[inner_slots].set(1)
    order = jax.random.permutation(key_rest, SLOTS).astype(jnp.int32)
    free_slots = jnp.argsort(order + taken * SLOTS, stable=True).astype(jnp.int32)
    local = jnp.arange(7, dtype=jnp.int32)
    inner_segments = jnp.concatenate([local, local + half])
    leaf_local = jnp.arange(half - 7, dtype=jnp.int32) + 7
    leaf_segments = jnp.concatenate([leaf_local, leaf_local + half])
    result = jnp.zeros((SLOTS,), jnp.int32).at[inner_segments].set(inner_slots)
    return result.at[leaf_segments].set(free_slots[:SLOTS - 14])


def draw_lengths(key, part):
    key = jax.random.fold_in(key, 9)
    drawn = jax.random.randint(key, (SLOTS,), SEG_LEN // 8, SEG_LEN + 1).astype(jnp.int32)
    return drawn.at[0].set(SEG_LEN).at[1].set(SEG_LEN // 8)


def with_spikes(entries, stream_key, source, target, blocks, factor):
    owner, partner = [(jnp.arange(entries.shape[position]) // (entries.shape[position] // blocks)).reshape([-1 if axis == position else 1 for axis in range(entries.ndim)]) for position in (source, target)]
    chosen = jax.random.permutation(stream_key, blocks)[partner]
    strong = (owner == chosen) | (owner == (partner + blocks // 2) % blocks)
    return jnp.where(strong, factor * entries, entries)


def levels(own_key, shape, cuts, least, top_value):
    factor_of, own = 1.0, jax.random.fold_in(own_key, 6)
    for position, shards_of in cuts:
        steps = jnp.exp(jax.random.uniform(jax.random.fold_in(own, position), (shards_of,), jnp.float32, least / len(cuts), top_value / len(cuts)))
        factor_of = factor_of * jnp.repeat(steps, shape[position] // shards_of).reshape([-1 if axis == position else 1 for axis in range(len(shape))])
    return factor_of


def normal_values(own_key, extent, width, bound, cuts=(), held_as=jnp.bfloat16):
    gain = levels(own_key, extent, cuts, -0.22, 0.18) if cuts else 1.0
    values = jax.random.normal(own_key, extent, jnp.float32) * width * gain
    return jnp.minimum(jnp.maximum(values, -bound), bound).astype(held_as)


def heavy_noise(stream_key, extent, width, bound, shards, heavy, kind=jnp.bfloat16):
    values = width * jax.random.normal(stream_key, extent, jnp.float32)
    if shards:
        values = values * levels(stream_key, extent, shards, -0.22, 0.18)
    return jnp.clip(with_spikes(values, jax.random.fold_in(stream_key, 3), *heavy), -bound, bound).astype(kind)


def setup_inputs(seed: int = 0) -> dict:
    key_list = jax.random.split(jax.random.key(seed), 8)
    hidden = heavy_noise(key_list[0], (SLOTS, SEG_LEN, D), 1.0, 6.0, ((0, 32),), (0, 2, 32, 2.75))
    kv_weight = normal_values(key_list[1], (2, D, KVH * HD), D ** -0.5, 0.078125, ((2, 8),))
    queries = draw_queries(jax.random.fold_in(key_list[7], 71), 0)
    out_grad = normal_values(key_list[3], (SLOTS, SEG_LEN, QH * HD), 1.0, 6.0, ((0, 32), (2, 8)))
    parents = draw_parents(jax.random.fold_in(key_list[7], 71), 0)
    placement = draw_placement(jax.random.fold_in(key_list[7], 71), 0)
    lengths = draw_lengths(jax.random.fold_in(key_list[7], 71), 0)
    return dict(hidden=hidden, kv_weight=kv_weight, queries=queries, out_grad=out_grad, parents=parents, placement=placement, lengths=lengths)


MASKED = -1e30


def chains(parents, placement, lengths, slot_count):
    slot_ids = jnp.arange(slot_count, dtype=jnp.int32)
    segment = jnp.zeros((slot_count,), jnp.int32).at[placement].set(slot_ids)
    members = []
    member_len = []
    for depth_level in range(DEPTH):
        usable = segment >= 0
        clamped = jnp.maximum(segment, 0)
        members.append(jnp.where(usable, placement[clamped], slot_ids))
        member_len.append(jnp.where(usable, lengths[clamped], 0))
        segment = jnp.where(usable, parents[clamped], -1)
    return jnp.stack(members, 1), jnp.stack(member_len, 1)


def allowed_mask(member_len, length):
    query_pos = jnp.arange(length, dtype=jnp.int32)[:, None]
    key_pos = jnp.arange(length, dtype=jnp.int32)[None, :]
    blocks = []
    for depth_level in range(DEPTH):
        inside = key_pos < member_len[depth_level]
        if depth_level == 0:
            inside = inside & (key_pos <= query_pos)
        blocks.append(jnp.broadcast_to(inside, (length, length)))
    return jnp.concatenate(blocks, 1) & (query_pos < member_len[0])


def attend(query_rows, key_rows, value_rows, grad_rows, allowed):
    length = query_rows.shape[0]
    key_count = key_rows.shape[0]
    kv_heads = key_rows.shape[1] // HD
    group_size = query_rows.shape[1] // HD // kv_heads
    scale = HD ** -0.5
    best = lax.Precision.HIGHEST
    query_f = query_rows.astype(jnp.float32).reshape(length, kv_heads, group_size, HD)
    key_f = key_rows.astype(jnp.float32).reshape(key_count, kv_heads, HD)
    value_f = value_rows.astype(jnp.float32).reshape(key_count, kv_heads, HD)
    grad_f = grad_rows.astype(jnp.float32).reshape(length, kv_heads, group_size, HD)
    scores = jnp.einsum('qhgd,khd->hgqk', query_f, key_f, precision=best) * scale
    usable = allowed[None, None]
    row_top = jnp.max(jnp.where(usable, scores, MASKED), -1, keepdims=True)
    weights = jnp.where(usable, jnp.exp(scores - row_top), 0.0)
    probs = weights / jnp.maximum(jnp.sum(weights, -1, keepdims=True), 1.0)
    probs_b = probs.astype(jnp.bfloat16)
    result = jnp.einsum('hgqk,khd->qhgd', probs_b.astype(jnp.float32), value_f, precision=best)
    result = result.reshape(length, kv_heads * group_size * HD).astype(jnp.bfloat16)
    dprobs = jnp.einsum('qhgd,khd->hgqk', grad_f, value_f, precision=best)
    delta = jnp.sum(probs * dprobs, -1, keepdims=True)
    score_grad = (probs * (dprobs - delta)).astype(jnp.bfloat16).astype(jnp.float32)
    query_grad = jnp.einsum('hgqk,khd->qhgd', score_grad, key_f, precision=best) * scale
    query_grad = query_grad.reshape(length, -1).astype(jnp.bfloat16)
    key_grad = jnp.einsum('hgqk,qhgd->khd', score_grad, query_f, precision=best) * scale
    value_grad = jnp.einsum('hgqk,qhgd->khd', probs_b.astype(jnp.float32), grad_f, precision=best)
    return result, query_grad, key_grad.reshape(key_count, -1), value_grad.reshape(key_count, -1)


def reference(hidden, kv_weight, queries, out_grad, parents, placement, lengths):
    kv_cols = KVH * HD
    flat_rows = hidden.reshape(SLOTS * SEG_LEN, D)
    key_rows = jnp.dot(flat_rows, kv_weight[0], preferred_element_type=jnp.float32)
    value_rows = jnp.dot(flat_rows, kv_weight[1], preferred_element_type=jnp.float32)
    key_rows = key_rows.reshape(SLOTS, SEG_LEN, kv_cols)
    value_rows = value_rows.reshape(SLOTS, SEG_LEN, kv_cols)
    members, member_len = chains(parents, placement, lengths, SLOTS)

    def slot_step(carry, slot_index):
        key_total, value_total = carry
        picked = members[slot_index]
        allowed = allowed_mask(member_len[slot_index], SEG_LEN)
        member_keys = key_rows[picked].reshape(DEPTH * SEG_LEN, kv_cols)
        member_values = value_rows[picked].reshape(DEPTH * SEG_LEN, kv_cols)
        result, query_grad, key_grad, value_grad = attend(queries[slot_index], member_keys, member_values, out_grad[slot_index], allowed)
        key_total = key_total.at[picked].add(key_grad.reshape(DEPTH, SEG_LEN, kv_cols))
        value_total = value_total.at[picked].add(value_grad.reshape(DEPTH, SEG_LEN, kv_cols))
        return (key_total, value_total), (result, query_grad)

    empty_grads = jnp.zeros((SLOTS, SEG_LEN, kv_cols), jnp.float32)
    totals, outputs = lax.scan(slot_step, (empty_grads, empty_grads), jnp.arange(SLOTS, dtype=jnp.int32))
    key_total_b = totals[0].astype(jnp.bfloat16).reshape(SLOTS * SEG_LEN, kv_cols)
    value_total_b = totals[1].astype(jnp.bfloat16).reshape(SLOTS * SEG_LEN, kv_cols)
    weight_grad = jnp.stack([
        jnp.dot(flat_rows.T, key_total_b, preferred_element_type=jnp.float32),
        jnp.dot(flat_rows.T, value_total_b, preferred_element_type=jnp.float32)])
    hidden_grad = jnp.dot(key_total_b, kv_weight[0].T, preferred_element_type=jnp.float32)
    hidden_grad = hidden_grad + jnp.dot(value_total_b, kv_weight[1].T, preferred_element_type=jnp.float32)
    hidden_grad = hidden_grad.astype(jnp.bfloat16).reshape(SLOTS, SEG_LEN, D)
    return outputs[0], outputs[1], hidden_grad, weight_grad
```

```python
import functools

import jax
import jax.numpy as jnp
from jax import lax
from jax.experimental import pallas as pl
from jax.experimental.pallas import tpu as pltpu
from jax.sharding import PartitionSpec as P

HD = 128
DEPTH = 4
NZ = 8
NY = 4
MASKED = -1e30
LOG2E = 1.4426950408889634
BF = jnp.bfloat16
F32 = jnp.float32
NT = (((1,), (1,)), ((), ()))


def over_core(x):
    return lax.ppermute(x, "dp", [(d, d ^ 1) for d in range(32)])


def over_xlo(x):
    return lax.ppermute(x, "dp", [(d, d ^ 2) for d in range(32)])


def over_z(x, step):
    return lax.ppermute(x, "dp", [(d, (d + 4 * step) % 32) for d in range(32)])


def over_y(x, step):
    return lax.ppermute(x, "mp", [(m, (m & 4) | ((m + step) & 3)) for m in range(8)])


def over_xhi(x):
    return lax.ppermute(x, "mp", [(m, m ^ 4) for m in range(8)])


def smem():
    return pl.BlockSpec(memory_space=pltpu.SMEM)


def vmem():
    return pl.BlockSpec(memory_space=pltpu.VMEM)


def project_kernel(ids, parents, placement, hidden, weight, own, sent, total, offset):
    step = pl.program_id(0)

    @pl.when(step == 0)
    def _():
        slot = ids[0] * 2 + 1

        def look(g, found):
            up = parents[g]
            hit = (up >= 0) & (placement[jnp.maximum(up, 0)] == slot)
            return jnp.where(hit, 1, found)

        offset[0] = lax.fori_loop(0, parents.shape[0], look, 0)

    both = jnp.concatenate([weight[0], weight[1]], axis=1)
    part = jnp.dot(hidden[...], both, preferred_element_type=F32)

    @pl.when(step == 0)
    def _():
        total[...] = part

    @pl.when(step > 0)
    def _():
        total[...] += part

    @pl.when(step == pl.num_programs(0) - 1)
    def _():
        rows = total[...]
        key = rows[:, :HD]
        high = key.astype(BF)
        rest = (key - high.astype(F32)).astype(BF)
        packed = jnp.concatenate([high, rest, rows[:, HD:].astype(BF)], axis=1)
        half = packed.shape[0] // 2
        own[0] = packed[:half]
        own[1] = packed[half:]
        sent[...] = own[offset[0]]


def project(ids, parents, placement, hidden, weight):
    rows, width = hidden.shape
    tile = 640
    return pl.pallas_call(
        project_kernel,
        grid=(width // tile,),
        in_specs=[
            smem(),
            smem(),
            smem(),
            pl.BlockSpec((rows, tile), lambda k: (0, k)),
            pl.BlockSpec((2, tile, HD), lambda k: (0, k, 0)),
        ],
        out_specs=[
            pl.BlockSpec((2, rows // 2, 3 * HD), lambda k: (0, 0, 0)),
            pl.BlockSpec((rows // 2, 3 * HD), lambda k: (0, 0)),
        ],
        out_shape=[
            jax.ShapeDtypeStruct((2, rows // 2, 3 * HD), BF),
            jax.ShapeDtypeStruct((rows // 2, 3 * HD), BF),
        ],
        scratch_shapes=[pltpu.VMEM((rows, 2 * HD), F32), pltpu.SMEM((1,), jnp.int32)],
        compiler_params=pltpu.CompilerParams(vmem_limit_bytes=32 << 20),
        cost_estimate=pl.CostEstimate(flops=2 * rows * width * 256, bytes_accessed=6 << 20, transcendentals=0),
        name="project",
    )(ids, parents, placement, hidden, weight)


def turn_kernel(ids, hidden, out):
    xlo, core = ids[2], ids[3]
    turned = hidden[...].T
    chunk = out.shape[3]
    for x in range(2):
        for c in range(2):
            at = (2 * x + c) * chunk
            out[jnp.bitwise_xor(core, c), jnp.bitwise_xor(xlo, x), 0] = turned[at : at + chunk]


def turn(ids, hidden):
    rows, width = hidden.shape
    chunk = width // 32
    return pl.pallas_call(
        turn_kernel,
        grid_spec=pltpu.PrefetchScalarGridSpec(
            num_scalar_prefetch=1,
            grid=(NZ,),
            in_specs=[pl.BlockSpec((rows, 4 * chunk), lambda s, ids: (0, lax.rem(ids[1] + s, NZ)))],
            out_specs=pl.BlockSpec((2, 2, 1, chunk, rows), lambda s, ids: (0, 0, s, 0, 0)),
        ),
        out_shape=jax.ShapeDtypeStruct((2, 2, NZ, chunk, rows), BF),
        compiler_params=pltpu.CompilerParams(vmem_limit_bytes=32 << 20),
        cost_estimate=pl.CostEstimate(flops=rows * width, bytes_accessed=6 << 20, transcendentals=0),
        name="turn",
    )(ids, hidden)


def attend_kernel(
    ids, parents, placement, lengths, queries, grads, own, near, far,
    out, query_grad, own_grad, back,
    keys, values, keys_t, values_t, bias, key_sum, value_sum, total,
):
    device, zed, xlo, core = ids[0], ids[1], ids[2], ids[3]
    count = parents.shape[0]
    length = queries.shape[1]
    scale = HD ** (-0.5)
    total[...] = jnp.zeros_like(total)
    row = lax.broadcasted_iota(jnp.int32, (length, length), 0)
    col = lax.broadcasted_iota(jnp.int32, (length, length), 1)
    for i in range(2):
        slot = device * 2 + i
        segment = lax.fori_loop(0, count, lambda g, f: jnp.where(placement[g] == slot, g, f), 0)
        own_len = lengths[segment]
        keys[0:length] = own[i, :, : 2 * HD]
        values[0:length] = own[i, :, 2 * HD :]
        bias[0:length] = jnp.where((row < own_len) & (row <= col), 0.0, MASKED)
        at = []
        for j in range(1, DEPTH):
            up = jnp.where(segment >= 0, parents[jnp.maximum(segment, 0)], -1)
            there = up >= 0
            upper = jnp.maximum(up, 0)
            holder = jnp.where(there, placement[upper] // 2, device)
            up_len = jnp.where(there, lengths[upper], 0)
            d_core = jnp.bitwise_xor(jnp.bitwise_and(holder, 1), core)
            d_xlo = jnp.bitwise_xor(jnp.bitwise_and(holder // 2, 1), xlo)
            behind = jnp.bitwise_and(zed - holder // 4, NZ - 1)
            ahead = jnp.bitwise_and(holder // 4 - zed, NZ - 1)
            part = slice(j * length, (j + 1) * length)

            @pl.when(d_core == 0)
            def _():
                keys[part] = near[d_xlo * NZ + behind, :, : 2 * HD]
                values[part] = near[d_xlo * NZ + behind, :, 2 * HD :]

            @pl.when(d_core == 1)
            def _():
                keys[part] = far[d_xlo * NZ + behind, :, : 2 * HD]
                values[part] = far[d_xlo * NZ + behind, :, 2 * HD :]

            bias[part] = jnp.where(row < up_len, 0.0, MASKED)
            at.append(d_core * 16 + d_xlo * NZ + ahead)
            segment = up
        keys_t[...] = keys[:, :HD].T
        values_t[...] = values[...].T
        valid = lax.broadcasted_iota(jnp.int32, (1, 2 * length), 1)
        valid = jnp.bitwise_and(valid, length - 1) < own_len
        for pair in range(queries.shape[2] // HD // 2):
            lo, mid, hi = 2 * pair * HD, (2 * pair + 1) * HD, (2 * pair + 2) * HD
            q2 = jnp.concatenate([queries[i, :, lo:mid], queries[i, :, mid:hi]], axis=0)
            g2 = jnp.concatenate([grads[i, :, lo:mid], grads[i, :, mid:hi]], axis=0)
            scores = lax.dot_general(
                keys[...], jnp.concatenate([q2, q2], axis=1), NT, preferred_element_type=F32
            )
            both = bias[...]
            scores = scores + jnp.concatenate([both, both], axis=1)
            top = jnp.max(scores, axis=0, keepdims=True)
            weights = jnp.exp2((scores - top) * (scale * LOG2E))
            inverse = 1.0 / jnp.maximum(jnp.sum(weights, axis=0, keepdims=True), 1.0)
            probs = weights * jnp.where(valid, inverse, 0.0)
            probs_b = probs.astype(BF)
            dprobs = lax.dot_general(values[...], g2, NT, preferred_element_type=F32)
            delta = jnp.sum(probs * dprobs, axis=0, keepdims=True)
            score_grad = (probs * (dprobs - delta)).astype(BF)
            dv = jnp.dot(probs_b, g2, preferred_element_type=F32)
            dk = jnp.dot(score_grad, q2, preferred_element_type=F32)
            if pair == 0:
                value_sum[...] = dv
                key_sum[...] = dk
            else:
                value_sum[...] += dv
                key_sum[...] += dk
            result = jnp.dot(values_t[...], probs_b, preferred_element_type=F32)
            dq = jnp.dot(keys_t[...], score_grad, preferred_element_type=F32) * scale
            out[i, :, lo:mid] = result[:, :length].T.astype(BF)
            out[i, :, mid:hi] = result[:, length:].T.astype(BF)
            query_grad[i, :, lo:mid] = dq[:, :length].T.astype(BF)
            query_grad[i, :, mid:hi] = dq[:, length:].T.astype(BF)
        own_grad[i, :, :HD] = key_sum[0:length] * scale
        own_grad[i, :, HD:] = value_sum[0:length]
        for j in range(1, DEPTH):
            part = slice(j * length, (j + 1) * length)
            total[at[j - 1], :, :HD] += key_sum[part] * scale
            total[at[j - 1], :, HD:] += value_sum[part]
    back[...] = total[...].astype(BF)


def attend(ids, parents, placement, lengths, queries, grads, own, near, far):
    _, length, cols = queries.shape
    return pl.pallas_call(
        attend_kernel,
        in_specs=[smem()] * 4 + [vmem()] * 5,
        out_specs=[vmem()] * 4,
        out_shape=[
            jax.ShapeDtypeStruct((2, length, cols), BF),
            jax.ShapeDtypeStruct((2, length, cols), BF),
            jax.ShapeDtypeStruct((2, length, 2 * HD), F32),
            jax.ShapeDtypeStruct((32, length, 2 * HD), BF),
        ],
        scratch_shapes=[
            pltpu.VMEM((DEPTH * length, 2 * HD), BF),
            pltpu.VMEM((DEPTH * length, HD), BF),
            pltpu.VMEM((HD, DEPTH * length), BF),
            pltpu.VMEM((HD, DEPTH * length), BF),
            pltpu.VMEM((DEPTH * length, length), F32),
            pltpu.VMEM((DEPTH * length, HD), F32),
            pltpu.VMEM((DEPTH * length, HD), F32),
            pltpu.VMEM((32, length, 2 * HD), F32),
        ],
        compiler_params=pltpu.CompilerParams(vmem_limit_bytes=48 << 20),
        cost_estimate=pl.CostEstimate(flops=3 << 30, bytes_accessed=10 << 20, transcendentals=1 << 20),
        name="attend",
    )(ids, parents, placement, lengths, queries, grads, own, near, far)


def weight_kernel(h0, h1, h2, h3, t0, t1, t2, t3, out):
    part = jnp.dot(h0[0], t0[...], preferred_element_type=F32)
    part += jnp.dot(h1[0], t1[...], preferred_element_type=F32)
    part += jnp.dot(h2[0], t2[...], preferred_element_type=F32)
    part += jnp.dot(h3[0], t3[...], preferred_element_type=F32)
    out[0] = part.astype(BF)


def weight_part(hid, tot):
    _, chunk, rows = hid[0].shape
    return pl.pallas_call(
        weight_kernel,
        grid=(NZ,),
        in_specs=[pl.BlockSpec((1, chunk, rows), lambda s: (s, 0, 0))] * 4
        + [pl.BlockSpec((rows, 2 * HD), lambda s: (0, 0))] * 4,
        out_specs=pl.BlockSpec((1, chunk, 2 * HD), lambda s: (s, 0, 0)),
        out_shape=jax.ShapeDtypeStruct((NZ, chunk, 2 * HD), BF),
        compiler_params=pltpu.CompilerParams(vmem_limit_bytes=32 << 20),
        cost_estimate=pl.CostEstimate(flops=2 << 28, bytes_accessed=4 << 20, transcendentals=0),
        name="weight_part",
    )(*hid, *tot)


def hidden_kernel(ids, w0, w1, w2, w3, t0, t1, t2, t3, out):
    total = None
    for w, t in ((w0, t0), (w1, t1), (w2, t2), (w3, t3)):
        both = jnp.concatenate([w[0, 0], w[1, 0]], axis=1)
        part = lax.dot_general(t[...], both, NT, preferred_element_type=F32)
        total = part if total is None else total + part
    out[0] = total.astype(BF)


def hidden_part(ids, weights, tot):
    rows = tot[0].shape[0]
    cols = weights[0].shape[2]
    return pl.pallas_call(
        hidden_kernel,
        grid_spec=pltpu.PrefetchScalarGridSpec(
            num_scalar_prefetch=1,
            grid=(2,),
            in_specs=[pl.BlockSpec((2, 1, cols, HD), lambda s, ids: (0, jnp.bitwise_xor(ids[4], s), 0, 0))] * 4
            + [pl.BlockSpec((rows, 2 * HD), lambda s, ids: (0, 0))] * 4,
            out_specs=pl.BlockSpec((1, rows, cols), lambda s, ids: (s, 0, 0)),
        ),
        out_shape=jax.ShapeDtypeStruct((2, rows, cols), BF),
        compiler_params=pltpu.CompilerParams(vmem_limit_bytes=32 << 20),
        cost_estimate=pl.CostEstimate(flops=2 << 28, bytes_accessed=4 << 20, transcendentals=0),
        name="hidden_part",
    )(ids, *weights, *tot)


def gather_blocks(block):
    steps = [block] + [over_z(block, s) for s in range(1, NZ)]
    crossed = [None] * NZ
    for group in ((0, 1, 7), (2, 6), (3, 4, 5)):
        moved = over_xlo(jnp.stack([steps[s] for s in group]))
        for n, s in enumerate(group):
            crossed[s] = moved[n]
    near = jnp.stack(steps + crossed)
    return near, over_core(near)


def scatter_blocks(blocks):
    half = blocks.shape[0] // 2
    first = blocks[:half].astype(F32) + over_core(blocks[half:]).astype(F32)
    first = first.astype(BF)
    second = first[:NZ].astype(F32) + over_xlo(first[NZ:]).astype(F32)
    ahead = second.astype(BF)
    total = second[0]
    for s in range(1, NZ):
        total = total + over_z(ahead[s], s).astype(F32)
    return total


def local(hidden, kv_weight, queries, out_grad, parents, placement, lengths):
    seg_dev, seg_len, width = hidden.shape
    device = lax.axis_index("dp")
    m = lax.axis_index("mp")
    zed, xlo, core = device // 4, (device // 2) % 2, device % 2
    xhi, y = m // 4, m % 4
    ids = jnp.stack([device, zed, xlo, core, xhi, y]).astype(jnp.int32)
    flat = hidden.reshape(seg_dev * seg_len, width)

    own, block = project(ids, parents, placement, flat, kv_weight)
    near, far = gather_blocks(block)

    by_chunk = kv_weight.reshape(2, 2, NY, width // 8, HD)

    def chunk_of(step):
        return lax.dynamic_index_in_dim(by_chunk, (y + step) % NY, 2, keepdims=False)

    weights = [chunk_of(0)] + [over_y(chunk_of(s), s) for s in range(1, NY)]

    turned = turn(ids, flat)
    pair = over_core(turned[1])
    hid = [turned[0, 0], pair[0], over_xlo(turned[0, 1]), over_xlo(pair[1])]

    attended, query_grad, own_grad, back = attend(
        ids, parents, placement, lengths, queries, out_grad, own, near, far
    )
    returned = scatter_blocks(back)

    seg = jnp.arange(parents.shape[0])
    mine = (parents >= 0) & (placement[jnp.maximum(parents, 0)] == device * 2 + 1)
    inner = jnp.any(mine).astype(jnp.int32)
    place = (jnp.arange(2) == inner)[:, None, None]
    total = own_grad + jnp.where(place, returned[None], 0.0)
    total_b = total.astype(BF).reshape(seg_dev * seg_len, 2 * HD)

    along_y = [total_b] + [over_y(total_b, s) for s in range(1, NY)]
    crossed = over_xlo(total_b)
    group = [total_b, over_core(total_b), crossed, over_core(crossed)]

    term = weight_part(hid, group)
    half = hidden_part(ids, weights, along_y)

    hidden_grad = (half[0].astype(F32) + over_xhi(half[1]).astype(F32)).astype(BF)
    hidden_grad = hidden_grad.reshape(seg_dev, seg_len, width // 8)
    weight_sum = term[0].astype(F32)
    for s in range(1, NZ):
        weight_sum = weight_sum + over_z(term[s], s).astype(F32)
    weight_grad = jnp.stack([weight_sum[:, :HD], weight_sum[:, HD:]])
    return (attended, query_grad, hidden_grad, weight_grad)


def solution(mesh):
    return jax.shard_map(
        local,
        mesh=mesh,
        in_specs=(
            P("dp", None, None),
            P(None, None, "mp"),
            P("dp", None, "mp"),
            P("dp", None, "mp"),
            P(),
            P(),
            P(),
        ),
        out_specs=(
            P("dp", None, "mp"),
            P("dp", None, "mp"),
            P("dp", None, "mp"),
            P(None, "dp", "mp"),
        ),
        check_vma=False,
    )
```

```python
import jax
import jax.numpy as jnp
from jax import lax
from jax.experimental import pallas as pl
from jax.experimental.pallas import tpu as pltpu
from jax.sharding import PartitionSpec as P

HD = 128
DEPTH = 4
NZ = 8
NY = 4
MASKED = -1e30
LOG2E = 1.4426950408889634
BF = jnp.bfloat16
F32 = jnp.float32
NT = (((1,), (1,)), ((), ()))


def over_core(x):
    return lax.ppermute(x, "dp", [(d, d ^ 1) for d in range(32)])


def over_xlo(x):
    return lax.ppermute(x, "dp", [(d, d ^ 2) for d in range(32)])


def along_z(x, steps):
    return lax.ppermute(
        x, "dp", [(d, (d + (4 * steps if d % 2 == 0 else -4 * steps)) % 32) for d in range(32)]
    )


def over_y(x, step):
    return lax.ppermute(x, "mp", [(m, (m & 4) | ((m + step) & 3)) for m in range(8)])


def over_xhi(x):
    return lax.ppermute(x, "mp", [(m, m ^ 4) for m in range(8)])


def bits(x, low, count):
    return jnp.bitwise_and(lax.shift_right_logical(x, jnp.int32(low)), (1 << count) - 1)


def carrier(ahead, core):
    middle = jnp.bitwise_and(ahead, 3) == 0
    who = jnp.where(middle, core, lax.shift_right_logical(ahead, jnp.int32(2)))
    steps = jnp.where(ahead > 4, NZ - ahead, ahead)
    other = jnp.bitwise_xor(core, who)
    place = jnp.where(steps == 4, 0, jnp.where(steps == 0, 7, 7 - 2 * steps + other))
    return who, place


def smem():
    return pl.BlockSpec(memory_space=pltpu.SMEM)


def vmem():
    return pl.BlockSpec(memory_space=pltpu.VMEM)


def cost(us):
    return pl.CostEstimate(flops=int(us * 1.1e9), bytes_accessed=1 << 10, transcendentals=0)


def project_kernel(
    parents, placement, hidden, weight,
    own, sent, pair, offset, tiles, w0, w1, w2, w3, h_sem, w_sem,
):
    y = bits(lax.axis_index("mp"), 0, 2)
    rows, tile = tiles.shape[1], tiles.shape[2]
    copies = []
    for step, out in enumerate((w0, w1, w2, w3)):
        for x in range(2):
            k = 2 * step + x
            at = x * NY + jnp.bitwise_and(y + step, NY - 1)
            part = pl.ds(pl.multiple_of(at * tile, 128), tile)
            h = pltpu.make_async_copy(hidden.at[:, part], tiles.at[at], h_sem.at[k])
            w = pltpu.make_async_copy(weight.at[:, part], out.at[:, x], w_sem.at[k])
            h.start()
            w.start()
            copies.append((h, w, at, out, x))
    slot = lax.axis_index("dp") * 2 + 1
    found = jnp.int32(0)
    for g in range(parents.shape[0]):
        up = parents[g]
        hit = (up >= 0) & (placement[jnp.maximum(up, 0)] == slot)
        found = jnp.where(hit, 1, found)
    offset[0] = found
    total = None
    for h, w, at, out, x in copies:
        h.wait()
        w.wait()
        both = jnp.concatenate([out[0, x], out[1, x]], axis=1)
        term = jnp.dot(tiles[at], both, preferred_element_type=F32)
        total = term if total is None else total + term
    key = total[:, :HD]
    high = key.astype(BF)
    rest = (key - high.astype(F32)).astype(BF)
    packed = jnp.concatenate([high, rest, total[:, HD:].astype(BF)], axis=1)
    own[0] = packed[: rows // 2]
    own[1] = packed[rows // 2 :]
    block = own[found]
    sent[...] = block
    pair[0] = block
    pair[1] = block


def project(parents, placement, hidden, weight):
    rows, width = hidden.shape
    count = 8
    hbm = pl.BlockSpec(memory_space=pltpu.HBM)
    return pl.pallas_call(
        project_kernel,
        in_specs=[smem(), smem(), hbm, hbm],
        out_specs=[vmem()] * 3 + [smem()] + [vmem()] * 5,
        out_shape=[
            pltpu.VMEM((2, rows // 2, 3 * HD), BF),
            pltpu.VMEM((rows // 2, 3 * HD), BF),
            pltpu.VMEM((2, rows // 2, 3 * HD), BF),
            jax.ShapeDtypeStruct((1,), jnp.int32),
            pltpu.VMEM((count, rows, width // count), BF),
        ]
        + [pltpu.VMEM((2, 2, width // count, HD), BF)] * 4,
        scratch_shapes=[pltpu.SemaphoreType.DMA((count,)), pltpu.SemaphoreType.DMA((count,))],
        compiler_params=pltpu.CompilerParams(vmem_limit_bytes=8 << 20),
        cost_estimate=cost(5),
        name="project",
    )(
        parents,
        placement,
        pltpu.with_memory_space_constraint(hidden, pltpu.HBM),
        pltpu.with_memory_space_constraint(weight, pltpu.HBM),
    )


def turn_kernel(tiles, here, to_xlo, to_core, turned):
    device = lax.axis_index("dp")
    zed, xlo, core = bits(device, 2, 3), bits(device, 1, 1), bits(device, 0, 1)
    chunk = here.shape[1]
    for tile in range(NZ):
        turned[tile] = tiles[tile].T.reshape(4, chunk, tiles.shape[1])
    for d_core, d_xlo, out in ((1, 0, to_core.at[0]), (1, 1, to_core.at[1]), (0, 1, to_xlo), (0, 0, here)):
        who = jnp.bitwise_xor(core, d_core)
        x = jnp.bitwise_xor(xlo, d_xlo)
        for place in range(NZ):
            steps = (4, 3, 3, 2, 2, 1, 1, 0)[place]
            other = (0, 0, 1, 0, 1, 0, 1, 0)[place]
            tile = jnp.bitwise_and(zed + jnp.where(who == 0, steps, NZ - steps), NZ - 1)
            out[place] = turned[tile, 2 * x + jnp.bitwise_xor(who, other)]


def turn(tiles):
    count, rows, wide = tiles.shape
    chunk = wide // 4
    return pl.pallas_call(
        turn_kernel,
        in_specs=[vmem()],
        out_specs=[vmem()] * 3,
        out_shape=[
            pltpu.VMEM((NZ, chunk, rows), BF),
            pltpu.VMEM((NZ, chunk, rows), BF),
            pltpu.VMEM((2, NZ, chunk, rows), BF),
        ],
        scratch_shapes=[pltpu.VMEM((count, 4, chunk, rows), BF)],
        compiler_params=pltpu.CompilerParams(vmem_limit_bytes=12 << 20),
        cost_estimate=cost(3),
        name="turn",
    )(tiles)


def attend_kernel(*refs):
    parents, placement, lengths, queries, grads, own = refs[:6]
    blocks = refs[6:26]
    probs_out, score_out, turned_out, own_grad, kept, sent = refs[26:32]
    key_rows, value_rows, bias, key_sum, value_sum, total, found = refs[32:]
    device = lax.axis_index("dp")
    zed, xlo, core = bits(device, 2, 3), bits(device, 1, 1), bits(device, 0, 1)
    count = parents.shape[0]
    length = queries.shape[1]
    scale = HD ** (-0.5)
    for i in range(2):
        slot = device * 2 + i
        segment = jnp.int32(0)
        for g in range(count):
            segment = jnp.where(placement[g] == slot, g, segment)
        found[8 * i] = lengths[segment]
        key_rows[4 * i] = own[i, :, : 2 * HD]
        value_rows[4 * i] = own[i, :, 2 * HD :]
        for j in range(1, DEPTH):
            up = jnp.where(segment >= 0, parents[jnp.maximum(segment, 0)], -1)
            there = up >= 0
            upper = jnp.maximum(up, 0)
            holder = jnp.where(there, bits(placement[upper], 1, 5), device)
            found[8 * i + j] = jnp.where(there, lengths[upper], 0)
            h_zed, h_core = bits(holder, 2, 3), bits(holder, 0, 1)
            d_xlo = jnp.bitwise_xor(bits(holder, 1, 1), xlo)
            who, place = carrier(jnp.bitwise_and(h_zed - zed, NZ - 1), h_core)
            found[8 * i + 4 + j] = jnp.where(who == core, 0, 16) + d_xlo * NZ + place
            who, place = carrier(jnp.bitwise_and(zed - h_zed, NZ - 1), h_core)
            found[16 + 4 * i + j] = jnp.where(who == core, 0, 16) + d_xlo * NZ + place
            segment = up

    def fetch(n, _):
        member = 4 * (n // 3) + n % 3 + 1
        at = found[16 + member]
        spot = jnp.bitwise_and(at, NZ - 1)
        for side in range(4):

            @pl.when(lax.shift_right_logical(at, jnp.int32(3)) == side)
            def _():
                for k, (first, many) in enumerate(((0, 1), (1, 2), (3, 2), (5, 2), (7, 1))):

                    @pl.when((spot >= first) & (spot < first + many))
                    def _():
                        ref = blocks[5 * side + k]
                        key_rows[member] = ref[spot - first, :, : 2 * HD]
                        value_rows[member] = ref[spot - first, :, 2 * HD :]

        return 0

    lax.fori_loop(0, 6, fetch, 0)
    total[...] = jnp.zeros_like(total)
    row = lax.broadcasted_iota(jnp.int32, (length, length), 0)
    col = lax.broadcasted_iota(jnp.int32, (length, length), 1)
    for i in range(2):
        own_len = found[8 * i]
        keys = key_rows[4 * i : 4 * i + 4].reshape(DEPTH * length, 2 * HD)
        values = value_rows[4 * i : 4 * i + 4].reshape(DEPTH * length, HD)
        bias[0:length] = jnp.where((row < own_len) & (row <= col), 0.0, MASKED)
        for j in range(1, DEPTH):
            bias[j * length : (j + 1) * length] = jnp.where(row < found[8 * i + j], 0.0, MASKED)
        turned_out[i, 0] = keys[:, :HD].T
        turned_out[i, 1] = values.T
        valid = lax.broadcasted_iota(jnp.int32, (1, 2 * length), 1)
        valid = jnp.bitwise_and(valid, length - 1) < own_len
        pairs = queries.shape[2] // HD // 2
        for pair in range(pairs):
            lo, mid, hi = 2 * pair * HD, (2 * pair + 1) * HD, (2 * pair + 2) * HD
            q2 = jnp.concatenate([queries[i, :, lo:mid], queries[i, :, mid:hi]], axis=0)
            g2 = jnp.concatenate([grads[i, :, lo:mid], grads[i, :, mid:hi]], axis=0)
            scores = lax.dot_general(
                keys, jnp.concatenate([q2, q2], axis=1), NT, preferred_element_type=F32
            )
            both = bias[...]
            scores = scores + jnp.concatenate([both, both], axis=1)
            top = jnp.max(scores, axis=0, keepdims=True)
            weights = jnp.exp2((scores - top) * (scale * LOG2E))
            inverse = 1.0 / jnp.maximum(jnp.sum(weights, axis=0, keepdims=True), 1.0)
            probs = weights * jnp.where(valid, inverse, 0.0)
            probs_b = probs.astype(BF)
            dprobs = lax.dot_general(values, g2, NT, preferred_element_type=F32)
            delta = jnp.sum(probs * dprobs, axis=0, keepdims=True)
            score_grad = (probs * (dprobs - delta)).astype(BF)
            probs_out[i * pairs + pair] = probs_b
            score_out[i * pairs + pair] = score_grad
            dv = jnp.dot(probs_b, g2, preferred_element_type=F32)
            dk = jnp.dot(score_grad, q2, preferred_element_type=F32)
            if pair == 0:
                value_sum[...] = dv
                key_sum[...] = dk
            else:
                value_sum[...] += dv
                key_sum[...] += dk
        own_grad[i, :, :HD] = key_sum[0:length] * scale
        own_grad[i, :, HD:] = value_sum[0:length]
        for j in range(1, DEPTH):
            part = slice(j * length, (j + 1) * length)
            at = found[8 * i + 4 + j]
            total[at, :, :HD] += key_sum[part] * scale
            total[at, :, HD:] += value_sum[part]
    kept[...] = total[0:16].astype(BF)
    sent[...] = total[16:32].astype(BF)


def attend(parents, placement, lengths, queries, grads, own, blocks):
    _, length, cols = queries.shape
    pairs = cols // HD
    return pl.pallas_call(
        attend_kernel,
        in_specs=[smem()] * 3 + [vmem()] * 23,
        out_specs=[vmem()] * 6,
        out_shape=[
            pltpu.VMEM((pairs, DEPTH * length, 2 * length), BF),
            pltpu.VMEM((pairs, DEPTH * length, 2 * length), BF),
            pltpu.VMEM((2, 2, HD, DEPTH * length), BF),
            pltpu.VMEM((2, length, 2 * HD), F32),
            pltpu.VMEM((16, length, 2 * HD), BF),
            pltpu.VMEM((16, length, 2 * HD), BF),
        ],
        scratch_shapes=[
            pltpu.VMEM((8, length, 2 * HD), BF),
            pltpu.VMEM((8, length, HD), BF),
            pltpu.VMEM((DEPTH * length, length), F32),
            pltpu.VMEM((DEPTH * length, HD), F32),
            pltpu.VMEM((DEPTH * length, HD), F32),
            pltpu.VMEM((32, length, 2 * HD), F32),
            pltpu.SMEM((24,), jnp.int32),
        ],
        compiler_params=pltpu.CompilerParams(vmem_limit_bytes=16 << 20),
        cost_estimate=cost(7),
        name="attend",
    )(parents, placement, lengths, queries, grads, own, *blocks)


def finish_kernel(probs, score_grad, turned, out, query_grad):
    scale = HD ** (-0.5)
    length = out.shape[1]
    pairs = out.shape[2] // HD // 2
    for i in range(2):
        for pair in range(pairs):
            lo, mid, hi = 2 * pair * HD, (2 * pair + 1) * HD, (2 * pair + 2) * HD
            result = jnp.dot(turned[i, 1], probs[i * pairs + pair], preferred_element_type=F32)
            dq = jnp.dot(turned[i, 0], score_grad[i * pairs + pair], preferred_element_type=F32) * scale
            out[i, :, lo:mid] = result[:, :length].T.astype(BF)
            out[i, :, mid:hi] = result[:, length:].T.astype(BF)
            query_grad[i, :, lo:mid] = dq[:, :length].T.astype(BF)
            query_grad[i, :, mid:hi] = dq[:, length:].T.astype(BF)


def finish(probs, score_grad, turned, shape):
    return pl.pallas_call(
        finish_kernel,
        in_specs=[vmem()] * 3,
        out_specs=[vmem()] * 2,
        out_shape=[jax.ShapeDtypeStruct(shape, BF)] * 2,
        compiler_params=pltpu.CompilerParams(vmem_limit_bytes=24 << 20),
        cost_estimate=cost(2),
        name="finish",
    )(probs, score_grad, turned)


def total_kernel(offset, own, first, second, out):
    back = first[...] + second[...].astype(F32)
    for i in range(2):
        out[i] = (own[i] + jnp.where(offset[0] == i, back, 0.0)).astype(BF)


def totals(offset, own, first, second):
    return pl.pallas_call(
        total_kernel,
        in_specs=[smem(), vmem(), vmem(), vmem()],
        out_specs=vmem(),
        out_shape=pltpu.VMEM(own.shape, BF),
        compiler_params=pltpu.CompilerParams(vmem_limit_bytes=8 << 20),
        name="totals",
    )(offset, own, first, second)


def weight_kernel(h0, h1, h2, h3, t0, t1, t2, t3, p43, p2, p1, p0):
    _, chunk, rows = h0.shape
    for ref, first, many in ((p43, 0, 3), (p2, 3, 2), (p1, 5, 2), (p0, 7, 1)):
        part = None
        for h, t in ((h0, t0), (h1, t1), (h2, t2), (h3, t3)):
            left = h[first : first + many].reshape(many * chunk, rows)
            term = jnp.dot(left, t[...], preferred_element_type=F32)
            part = term if part is None else part + term
        ref[...] = part.reshape(many, chunk, part.shape[1]).astype(ref.dtype)


def weight_part(hid, tot):
    _, chunk, rows = hid[0].shape
    cols = tot[0].shape[1]
    return pl.pallas_call(
        weight_kernel,
        in_specs=[vmem()] * 8,
        out_specs=[vmem()] * 4,
        out_shape=[pltpu.VMEM((many, chunk, cols), BF if many == 3 else F32) for many in (3, 2, 2, 1)],
        compiler_params=pltpu.CompilerParams(vmem_limit_bytes=12 << 20),
        cost_estimate=cost(2),
        name="weight_part",
    )(*hid, *tot)


def hidden_kernel(w0, w1, w2, w3, t0, t1, t2, t3, mine, other):
    xhi = bits(lax.axis_index("mp"), 2, 1)
    for ref, d in ((other, 1), (mine, 0)):
        total = None
        at = jnp.bitwise_xor(xhi, d)
        for w, t in ((w0, t0), (w1, t1), (w2, t2), (w3, t3)):
            both = jnp.concatenate([w[0, at], w[1, at]], axis=1)
            part = lax.dot_general(t[...], both, NT, preferred_element_type=F32)
            total = part if total is None else total + part
        ref[...] = total.astype(ref.dtype)


def hidden_part(weights, tot):
    rows = tot[0].shape[0]
    cols = weights[0].shape[2]
    return pl.pallas_call(
        hidden_kernel,
        in_specs=[vmem()] * 8,
        out_specs=[vmem()] * 2,
        out_shape=[pltpu.VMEM((rows, cols), F32), pltpu.VMEM((rows, cols), BF)],
        compiler_params=pltpu.CompilerParams(vmem_limit_bytes=12 << 20),
        cost_estimate=cost(2),
        name="hidden_part",
    )(*weights, *tot)


def local(hidden, kv_weight, queries, out_grad, parents, placement, lengths):
    seg_dev, seg_len, width = hidden.shape
    flat = hidden.reshape(seg_dev * seg_len, width)

    own, block, pair, offset, tiles, w0, w1, w2, w3 = project(parents, placement, flat, kv_weight)

    x0 = over_xlo(block)
    pair = pair.at[1].set(over_core(block))
    z2, z1 = along_z(pair, 2), along_z(pair, 1)
    z3, z4 = along_z(z2, 1), along_z(z2[0], 2)

    h0, to_xlo, to_core = turn(tiles)
    from_core = over_core(to_core)
    h2 = over_xlo(to_xlo)
    w1, w3 = over_y(w1, 1), over_y(w3, 3)

    x1, x2, x3, x4 = over_xlo(z1), over_xlo(z2), over_xlo(z3), over_xlo(z4)
    near = [z4[None], z3, z2, z1, block[None], x4[None], x3, x2, x1, x0[None]]
    far = [over_core(v) for v in near]
    h1, h3 = from_core[0], from_core[1]
    h3, w2 = over_xlo(h3), over_y(w2, 2)

    probs, score_grad, member_t, own_grad, kept, sent = attend(
        parents, placement, lengths, queries, out_grad, own, near + far
    )

    came = over_core(sent)

    def both(first, last):
        return kept[first:last].astype(F32) + came[first:last].astype(F32)

    y1 = over_xlo(both(8, 11).astype(BF))
    y2 = over_xlo(both(11, 16).astype(BF))
    attended, query_grad = finish(probs, score_grad, member_t, queries.shape)
    r43 = along_z((both(0, 3) + y1.astype(F32)).astype(BF), 2).astype(F32)
    s2 = both(3, 8) + y2.astype(F32)
    r2 = along_z(jnp.stack([s2[0] + r43[0], s2[1]]).astype(BF), 2)
    r1 = along_z((s2[2:4] + r43[1:3]).astype(BF), 1)
    for_me = s2[4] + r2[0].astype(F32) + r1[0].astype(F32)
    for_sibling = (r2[1].astype(F32) + r1[1].astype(F32)).astype(BF)
    for_sibling, h2, w1, w3 = lax.optimization_barrier((for_sibling, h2, w1, w3))
    total = totals(offset, own_grad, for_me, over_core(for_sibling))
    total = total.reshape(seg_dev * seg_len, 2 * HD)

    crossed = over_xlo(total)
    group = [total, over_core(total), crossed, over_core(crossed)]
    along_y = [total] + [over_y(total, s) for s in range(1, NY)]

    p43, p2, p1, p0 = weight_part([h0, h1, h2, h3], group)
    p43 = along_z(p43, 2).astype(F32)
    p2 = along_z(jnp.stack([p2[0] + p43[0], p2[1]]).astype(BF), 2)
    p1 = along_z((p1 + p43[1:3]).astype(BF), 1)
    mine, other = hidden_part([w0, w1, w2, w3], along_y)
    hidden_grad = (mine + over_xhi(other).astype(F32)).astype(BF)
    hidden_grad = hidden_grad.reshape(seg_dev, seg_len, width // 8)

    weight_sum = p0[0] + p2[0].astype(F32) + p1[0].astype(F32)
    weight_sibling = (p2[1].astype(F32) + p1[1].astype(F32)).astype(BF)
    weight_sum = weight_sum + over_core(weight_sibling).astype(F32)
    weight_grad = jnp.stack([weight_sum[:, :HD], weight_sum[:, HD:]])
    return (attended, query_grad, hidden_grad, weight_grad)


def solution(mesh):
    return jax.shard_map(
        local,
        mesh=mesh,
        in_specs=(
            P("dp", None, None),
            P(None, None, "mp"),
            P("dp", None, "mp"),
            P("dp", None, "mp"),
            P(),
            P(),
            P(),
        ),
        out_specs=(
            P("dp", None, "mp"),
            P("dp", None, "mp"),
            P("dp", None, "mp"),
            P(None, "dp", "mp"),
        ),
        check_vma=False,
    )
```

```python
import jax
import jax.numpy as jnp
from jax import lax
from jax.experimental import pallas as pl
from jax.experimental.pallas import tpu as pltpu
from jax.sharding import PartitionSpec as P

HD = 128
DEPTH = 4
NZ = 8
NY = 4
MASKED = -1e30
LOG2E = 1.4426950408889634
BF = jnp.bfloat16
F32 = jnp.float32
NT = (((1,), (1,)), ((), ()))


def over_core(x):
    return lax.ppermute(x, "dp", [(d, d ^ 1) for d in range(32)])


def over_xlo(x):
    return lax.ppermute(x, "dp", [(d, d ^ 2) for d in range(32)])


def along_z(x, steps):
    return lax.ppermute(
        x, "dp", [(d, (d + (4 * steps if d % 2 == 0 else -4 * steps)) % 32) for d in range(32)]
    )


def over_y(x, step):
    return lax.ppermute(x, "mp", [(m, (m & 4) | ((m + step) & 3)) for m in range(8)])


def along_y(x):
    pairs = []
    for d in range(32):
        for m in range(8):
            to = (m & 4) | ((m + (1 if d % 2 == 0 else -1)) & 3)
            pairs.append((d * 8 + m, d * 8 + to))
    return lax.ppermute(x, ("dp", "mp"), pairs)


def over_xhi(x):
    return lax.ppermute(x, "mp", [(m, m ^ 4) for m in range(8)])


def bits(x, low, count):
    return jnp.bitwise_and(lax.shift_right_logical(x, jnp.int32(low)), (1 << count) - 1)


def carrier(ahead, core):
    middle = jnp.bitwise_and(ahead, 3) == 0
    who = jnp.where(middle, core, lax.shift_right_logical(ahead, jnp.int32(2)))
    steps = jnp.where(ahead > 4, NZ - ahead, ahead)
    other = jnp.bitwise_xor(core, who)
    place = jnp.where(steps == 4, 0, jnp.where(steps == 0, 7, 7 - 2 * steps + other))
    return who, place


def smem():
    return pl.BlockSpec(memory_space=pltpu.SMEM)


def vmem():
    return pl.BlockSpec(memory_space=pltpu.VMEM)


def cost(us):
    return pl.CostEstimate(flops=int(us * 1.1e9) if us > 6 else 1 << 10, bytes_accessed=1 << 10, transcendentals=0)


def project_kernel(
    parents, placement, hidden, weight,
    own, sent, pair, offset, tiles, w0, wa, wc, h_sem, w_sem, wb, wd, ups, places, i_sem,
):
    lists = [
        pltpu.make_async_copy(parents, ups, i_sem.at[0]),
        pltpu.make_async_copy(placement, places, i_sem.at[1]),
    ]
    for copy in lists:
        copy.start()
    y = bits(lax.axis_index("mp"), 0, 2)
    rows, tile = tiles.shape[1], tiles.shape[2]
    copies = []
    core = bits(lax.axis_index("dp"), 0, 1)
    near = jnp.where(core == 0, 1, NY - 1)
    for step, steps in enumerate((0, near, 2, NY - near)):
        for x in range(2):
            k = 2 * step + x
            at = x * NY + jnp.bitwise_and(y + steps, NY - 1)
            part = pl.ds(pl.multiple_of(at * tile, 128), tile)
            h = pltpu.make_async_copy(hidden.at[:, part], tiles.at[at], h_sem.at[k])
            if step == 2:
                first = pltpu.make_async_copy(weight.at[core, part], wc.at[x], w_sem.at[k])
                last = pltpu.make_async_copy(weight.at[1 - core, part], wd.at[x], w_sem.at[8 + x])
                w = (first, last)
            else:
                out = {0: w0, 1: wa, 3: wb}[step]
                w = (pltpu.make_async_copy(weight.at[:, part], out.at[:, x], w_sem.at[k]),)
            for copy in (h, *w):
                copy.start()
            copies.append((h, w, at, step, x))
    for copy in lists:
        copy.wait()
    slot = lax.axis_index("dp") * 2 + 1
    found = jnp.int32(0)
    for g in range(parents.shape[0]):
        up = ups[g]
        hit = (up >= 0) & (places[jnp.maximum(up, 0)] == slot)
        found = jnp.where(hit, 1, found)
    offset[0] = found
    total = None
    for h, w, at, step, x in copies:
        for copy in (h, *w):
            copy.wait()
        if step == 2:
            flip = core == 1
            first, last = wc[x], wd[x]
            both = jnp.concatenate([jnp.where(flip, last, first), jnp.where(flip, first, last)], axis=1)
        else:
            out = {0: w0, 1: wa, 3: wb}[step]
            both = jnp.concatenate([out[0, x], out[1, x]], axis=1)
        term = jnp.dot(tiles[at], both, preferred_element_type=F32)
        total = term if total is None else total + term
    key = total[:, :HD]
    high = key.astype(BF)
    rest = (key - high.astype(F32)).astype(BF)
    packed = jnp.concatenate([high, rest, total[:, HD:].astype(BF)], axis=1)
    own[0] = packed[: rows // 2]
    own[1] = packed[rows // 2 :]
    block = own[found]
    sent[...] = block
    pair[0] = block
    pair[1] = block


def project(parents, placement, hidden, weight):
    rows, width = hidden.shape
    count = 8
    hbm = pl.BlockSpec(memory_space=pltpu.HBM)
    return pl.pallas_call(
        project_kernel,
        in_specs=[hbm] * 4,
        out_specs=[vmem()] * 3 + [smem()] + [vmem()] * 4,
        out_shape=[
            pltpu.VMEM((2, rows // 2, 3 * HD), BF),
            pltpu.VMEM((rows // 2, 3 * HD), BF),
            pltpu.VMEM((2, rows // 2, 3 * HD), BF),
            jax.ShapeDtypeStruct((1,), jnp.int32),
            pltpu.VMEM((count, rows, width // count), BF),
        ]
        + [pltpu.VMEM((2, 2, width // count, HD), BF)] * 2
        + [pltpu.VMEM((2, width // count, HD), BF)],
        scratch_shapes=[
            pltpu.SemaphoreType.DMA((count,)),
            pltpu.SemaphoreType.DMA((count + 2,)),
            pltpu.VMEM((2, 2, width // count, HD), BF),
            pltpu.VMEM((2, width // count, HD), BF),
            pltpu.SMEM(parents.shape, jnp.int32),
            pltpu.SMEM(parents.shape, jnp.int32),
            pltpu.SemaphoreType.DMA((2,)),
        ],
        compiler_params=pltpu.CompilerParams(vmem_limit_bytes=8 << 20),
        cost_estimate=cost(5),
        name="project",
    )(*(pltpu.with_memory_space_constraint(v, pltpu.HBM) for v in (parents, placement, hidden, weight)))


def turn_kernel(tiles, here, to_xlo, away, to_core, turned):
    device = lax.axis_index("dp")
    zed, xlo, core = bits(device, 2, 3), bits(device, 1, 1), bits(device, 0, 1)
    chunk = here.shape[1]
    for tile in range(NZ):
        turned[tile] = tiles[tile].T.reshape(4, chunk, tiles.shape[1])
    early = to_xlo.shape[1]
    for d_core, d_xlo, out in ((1, 0, to_core.at[0]), (1, 1, to_core.at[1]), (0, 1, to_xlo.at[0]), (0, 0, here)):
        who = jnp.bitwise_xor(core, d_core)
        x = jnp.bitwise_xor(xlo, d_xlo)
        for place in range(NZ):
            steps = (4, 3, 3, 2, 2, 1, 1, 0)[place]
            other = (0, 0, 1, 0, 1, 0, 1, 0)[place]
            tile = jnp.bitwise_and(zed + jnp.where(who == 0, steps, NZ - steps), NZ - 1)
            piece = turned[tile, 2 * x + jnp.bitwise_xor(who, other)]
            if (d_core, d_xlo) == (0, 1) and place >= early:
                away[place - early] = piece
            else:
                out[place] = piece


def turn(tiles):
    count, rows, wide = tiles.shape
    chunk = wide // 4
    return pl.pallas_call(
        turn_kernel,
        in_specs=[vmem()],
        out_specs=[vmem()] * 4,
        out_shape=[
            pltpu.VMEM((NZ, chunk, rows), BF),
            pltpu.VMEM((2, 5, chunk, rows), BF),
            pltpu.VMEM((3, chunk, rows), BF),
            pltpu.VMEM((2, NZ, chunk, rows), BF),
        ],
        scratch_shapes=[pltpu.VMEM((count, 4, chunk, rows), BF)],
        compiler_params=pltpu.CompilerParams(vmem_limit_bytes=12 << 20),
        cost_estimate=cost(3),
        name="turn",
    )(tiles)


def attend_kernel(*refs):
    parents, placement, lengths, queries, grads, own = refs[:6]
    blocks = refs[6:26]
    probs_out, score_out, turned_out, own_grad, kept, sent = refs[26:32]
    key_rows, value_rows, bias, key_sum, value_sum, total, found = refs[32:]
    device = lax.axis_index("dp")
    zed, xlo, core = bits(device, 2, 3), bits(device, 1, 1), bits(device, 0, 1)
    count = parents.shape[0]
    length = queries.shape[1]
    scale = HD ** (-0.5)
    for i in range(2):
        slot = device * 2 + i
        segment = jnp.int32(0)
        for g in range(count):
            segment = jnp.where(placement[g] == slot, g, segment)
        found[8 * i] = lengths[segment]
        key_rows[4 * i] = own[i, :, : 2 * HD]
        value_rows[4 * i] = own[i, :, 2 * HD :]
        for j in range(1, DEPTH):
            up = jnp.where(segment >= 0, parents[jnp.maximum(segment, 0)], -1)
            there = up >= 0
            upper = jnp.maximum(up, 0)
            holder = jnp.where(there, bits(placement[upper], 1, 5), device)
            found[8 * i + j] = jnp.where(there, lengths[upper], 0)
            h_zed, h_core = bits(holder, 2, 3), bits(holder, 0, 1)
            d_xlo = jnp.bitwise_xor(bits(holder, 1, 1), xlo)
            who, place = carrier(jnp.bitwise_and(h_zed - zed, NZ - 1), h_core)
            found[8 * i + 4 + j] = jnp.where(who == core, 0, 16) + d_xlo * NZ + place
            who, place = carrier(jnp.bitwise_and(zed - h_zed, NZ - 1), h_core)
            found[16 + 4 * i + j] = jnp.where(who == core, 0, 16) + d_xlo * NZ + place
            segment = up

    def fetch(n, _):
        member = 4 * (n // 3) + n % 3 + 1
        at = found[16 + member]
        spot = jnp.bitwise_and(at, NZ - 1)
        for side in range(4):

            @pl.when(lax.shift_right_logical(at, jnp.int32(3)) == side)
            def _():
                for k, (first, many) in enumerate(((0, 1), (1, 2), (3, 2), (5, 2), (7, 1))):

                    @pl.when((spot >= first) & (spot < first + many))
                    def _():
                        ref = blocks[5 * side + k]
                        key_rows[member] = ref[spot - first, :, : 2 * HD]
                        value_rows[member] = ref[spot - first, :, 2 * HD :]

        return 0

    lax.fori_loop(0, 6, fetch, 0)
    total[...] = jnp.zeros_like(total)
    row = lax.broadcasted_iota(jnp.int32, (length, length), 0)
    col = lax.broadcasted_iota(jnp.int32, (length, length), 1)
    for i in range(2):
        own_len = found[8 * i]
        keys = key_rows[4 * i : 4 * i + 4].reshape(DEPTH * length, 2 * HD)
        values = value_rows[4 * i : 4 * i + 4].reshape(DEPTH * length, HD)
        bias[0:length] = jnp.where((row < own_len) & (row <= col), 0.0, MASKED)
        for j in range(1, DEPTH):
            bias[j * length : (j + 1) * length] = jnp.where(row < found[8 * i + j], 0.0, MASKED)
        turned_out[i, 0] = keys[:, :HD].T
        turned_out[i, 1] = values.T
        valid = lax.broadcasted_iota(jnp.int32, (1, 2 * length), 1)
        valid = jnp.bitwise_and(valid, length - 1) < own_len
        pairs = queries.shape[2] // HD // 2
        for pair in range(pairs):
            lo, mid, hi = 2 * pair * HD, (2 * pair + 1) * HD, (2 * pair + 2) * HD
            q2 = jnp.concatenate([queries[i, :, lo:mid], queries[i, :, mid:hi]], axis=0)
            g2 = jnp.concatenate([grads[i, :, lo:mid], grads[i, :, mid:hi]], axis=0)
            scores = lax.dot_general(
                keys, jnp.concatenate([q2, q2], axis=1), NT, preferred_element_type=F32
            )
            both = bias[...]
            scores = scores + jnp.concatenate([both, both], axis=1)
            top = jnp.max(scores, axis=0, keepdims=True)
            weights = jnp.exp2((scores - top) * (scale * LOG2E))
            inverse = 1.0 / jnp.maximum(jnp.sum(weights, axis=0, keepdims=True), 1.0)
            probs = weights * jnp.where(valid, inverse, 0.0)
            probs_b = probs.astype(BF)
            dprobs = lax.dot_general(values, g2, NT, preferred_element_type=F32)
            delta = jnp.sum(probs * dprobs, axis=0, keepdims=True)
            score_grad = (probs * (dprobs - delta)).astype(BF)
            probs_out[i * pairs + pair] = probs_b
            score_out[i * pairs + pair] = score_grad
            dv = jnp.dot(probs_b, g2, preferred_element_type=F32)
            dk = jnp.dot(score_grad, q2, preferred_element_type=F32)
            if pair == 0:
                value_sum[...] = dv
                key_sum[...] = dk
            else:
                value_sum[...] += dv
                key_sum[...] += dk
        own_grad[i, :, :HD] = key_sum[0:length] * scale
        own_grad[i, :, HD:] = value_sum[0:length]
        for j in range(1, DEPTH):
            part = slice(j * length, (j + 1) * length)
            at = found[8 * i + 4 + j]
            total[at, :, :HD] += key_sum[part] * scale
            total[at, :, HD:] += value_sum[part]
    kept[...] = total[0:16].astype(BF)
    sent[...] = total[16:32].astype(BF)


def attend(parents, placement, lengths, queries, grads, own, blocks):
    _, length, cols = queries.shape
    pairs = cols // HD
    return pl.pallas_call(
        attend_kernel,
        in_specs=[smem()] * 3 + [vmem()] * 23,
        out_specs=[vmem()] * 6,
        out_shape=[
            pltpu.VMEM((pairs, DEPTH * length, 2 * length), BF),
            pltpu.VMEM((pairs, DEPTH * length, 2 * length), BF),
            pltpu.VMEM((2, 2, HD, DEPTH * length), BF),
            pltpu.VMEM((2, length, 2 * HD), F32),
        ]
        + [pltpu.VMEM((16, length, 2 * HD), BF)] * 2,
        scratch_shapes=[
            pltpu.VMEM((8, length, 2 * HD), BF),
            pltpu.VMEM((8, length, HD), BF),
            pltpu.VMEM((DEPTH * length, length), F32),
            pltpu.VMEM((DEPTH * length, HD), F32),
            pltpu.VMEM((DEPTH * length, HD), F32),
            pltpu.VMEM((32, length, 2 * HD), F32),
            pltpu.SMEM((24,), jnp.int32),
        ],
        compiler_params=pltpu.CompilerParams(vmem_limit_bytes=16 << 20),
        cost_estimate=cost(7),
        name="attend",
    )(parents, placement, lengths, queries, grads, own, *blocks)


def finish_kernel(probs, score_grad, turned, out, query_grad):
    scale = HD ** (-0.5)
    length = out.shape[1]
    pairs = out.shape[2] // HD // 2
    for i in range(2):
        for pair in range(pairs):
            lo, mid, hi = 2 * pair * HD, (2 * pair + 1) * HD, (2 * pair + 2) * HD
            result = jnp.dot(turned[i, 1], probs[i * pairs + pair], preferred_element_type=F32)
            dq = jnp.dot(turned[i, 0], score_grad[i * pairs + pair], preferred_element_type=F32) * scale
            out[i, :, lo:mid] = result[:, :length].T.astype(BF)
            out[i, :, mid:hi] = result[:, length:].T.astype(BF)
            query_grad[i, :, lo:mid] = dq[:, :length].T.astype(BF)
            query_grad[i, :, mid:hi] = dq[:, length:].T.astype(BF)


def finish(probs, score_grad, turned, shape):
    return pl.pallas_call(
        finish_kernel,
        in_specs=[vmem()] * 3,
        out_specs=[vmem()] * 2,
        out_shape=[jax.ShapeDtypeStruct(shape, BF)] * 2,
        compiler_params=pltpu.CompilerParams(vmem_limit_bytes=24 << 20),
        cost_estimate=cost(2),
        name="finish",
    )(probs, score_grad, turned)


def total_kernel(offset, own, first, second, out):
    back = first[...] + second[...].astype(F32)
    for i in range(2):
        out[i] = (own[i] + jnp.where(offset[0] == i, back, 0.0)).astype(BF)


def totals(offset, own, first, second):
    return pl.pallas_call(
        total_kernel,
        in_specs=[smem(), vmem(), vmem(), vmem()],
        out_specs=vmem(),
        out_shape=pltpu.VMEM(own.shape, BF),
        compiler_params=pltpu.CompilerParams(vmem_limit_bytes=8 << 20),
        name="totals",
    )(offset, own, first, second)


def far_kernel(here, came, crossed, t0, t1, t2, t3, p43, p2):
    chunk, rows = here.shape[1:]
    for ref, first, many in ((p43, 0, 3), (p2, 3, 2)):
        part = None
        for h, t in ((here, t0), (came.at[0], t1), (crossed.at[0], t2), (crossed.at[1], t3)):
            left = h[first : first + many].reshape(many * chunk, rows)
            term = jnp.dot(left, t[...], preferred_element_type=F32)
            part = term if part is None else part + term
        ref[...] = part.reshape(many, chunk, part.shape[1]).astype(ref.dtype)


def far_part(here, came, crossed, tot):
    chunk = here.shape[1]
    cols = tot[0].shape[1]
    return pl.pallas_call(
        far_kernel,
        in_specs=[vmem()] * 7,
        out_specs=[vmem()] * 2,
        out_shape=[pltpu.VMEM((3, chunk, cols), BF), pltpu.VMEM((2, chunk, cols), F32)],
        compiler_params=pltpu.CompilerParams(vmem_limit_bytes=12 << 20),
        cost_estimate=cost(1),
        name="far_part",
    )(here, came, crossed, *tot)


def close_kernel(here, came, away, t0, t1, mine, other):
    many, chunk, rows = away.shape
    first = here.shape[0] - many
    for ref, own, sibling in (
        (other, away[...], came[1, first:]),
        (mine, here[first:], came[0, first:]),
    ):
        part = jnp.dot(own.reshape(many * chunk, rows), t0[...], preferred_element_type=F32)
        part += jnp.dot(sibling.reshape(many * chunk, rows), t1[...], preferred_element_type=F32)
        ref[...] = part.reshape(ref.shape).astype(ref.dtype)


def close_part(here, came, away, t0, t1):
    shape = (*away.shape[:2], t0.shape[1])
    return pl.pallas_call(
        close_kernel,
        in_specs=[vmem()] * 5,
        out_specs=[vmem()] * 2,
        out_shape=[pltpu.VMEM(shape, F32), pltpu.VMEM(shape, BF)],
        compiler_params=pltpu.CompilerParams(vmem_limit_bytes=12 << 20),
        cost_estimate=cost(1),
        name="close_part",
    )(here, came, away, t0, t1)


def hidden_kernel(w0, wa, wb, wc, wd, t0, t1, t2, t3, mine, other, other2):
    xhi = bits(lax.axis_index("mp"), 2, 1)
    half = other.shape[0]
    for d in (1, 0):
        total = None
        at = jnp.bitwise_xor(xhi, d)
        flip = bits(lax.axis_index("dp"), 0, 1) == 1
        behind, ahead = t1[...], t3[...]
        pairs = (
            (w0[0, at], w0[1, at], t0[...]),
            (wa[0, at], wa[1, at], jnp.where(flip, ahead, behind)),
            (wb[0, at], wb[1, at], jnp.where(flip, behind, ahead)),
            (jnp.where(flip, wd[at], wc[at]), jnp.where(flip, wc[at], wd[at]), t2[...]),
        )
        for key, value, t in pairs:
            both = jnp.concatenate([key, value], axis=1)
            part = lax.dot_general(t, both, NT, preferred_element_type=F32)
            total = part if total is None else total + part
        if d:
            other[...] = total[:half].astype(BF)
            other2[...] = total[half:].astype(BF)
        else:
            mine[...] = total


def hidden_part(weights, tot):
    rows = tot[0].shape[0]
    cols = weights[0].shape[2]
    return pl.pallas_call(
        hidden_kernel,
        in_specs=[vmem()] * 9,
        out_specs=[vmem()] * 3,
        out_shape=[pltpu.VMEM((rows, cols), F32)] + [pltpu.VMEM((rows // 2, cols), BF)] * 2,
        compiler_params=pltpu.CompilerParams(vmem_limit_bytes=12 << 20),
        cost_estimate=cost(2),
        name="hidden_part",
    )(*weights, *tot)


def local(hidden, kv_weight, queries, out_grad, parents, placement, lengths):
    seg_dev, seg_len, width = hidden.shape
    flat = hidden.reshape(seg_dev * seg_len, width)

    own, block, pair, offset, tiles, w0, wa, wc = project(parents, placement, flat, kv_weight)

    x0 = over_xlo(block)
    pair = pair.at[1].set(over_core(block))
    z2, z1 = along_z(pair, 2), along_z(pair, 1)
    z3, z4 = along_z(z2, 1), along_z(z2[0], 2)

    h0, to_xlo, away, to_core = turn(tiles)
    from_core = over_core(to_core)
    to_xlo = to_xlo.at[1].set(from_core[1, :5])

    x1, x2 = over_xlo(z1), over_xlo(z2)
    z3, x1 = lax.optimization_barrier((z3, x1))
    z4, x2 = lax.optimization_barrier((z4, x2))
    x3, x4 = over_xlo(z3), over_xlo(z4)
    near = [z4[None], z3, z2, z1, block[None], x4[None], x3, x2, x1, x0[None]]
    far = [over_core(v) for v in near]

    probs, score_grad, member_t, own_grad, kept, sent = attend(
        parents, placement, lengths, queries, out_grad, own, near + far
    )

    came = over_core(sent)

    def both(first, last):
        return kept[first:last].astype(F32) + came[first:last].astype(F32)

    y1 = over_xlo(both(8, 11).astype(BF))
    y2 = over_xlo(both(11, 16).astype(BF))
    attended, query_grad = finish(probs, score_grad, member_t, queries.shape)
    y1, to_xlo = lax.optimization_barrier((y1, to_xlo))
    h23 = over_xlo(to_xlo)
    r43 = along_z((both(0, 3) + y1.astype(F32)).astype(BF), 2).astype(F32)
    s2 = both(3, 8) + y2.astype(F32)
    r2 = along_z(jnp.stack([s2[0] + r43[0], s2[1]]).astype(BF), 2)
    r1 = along_z((s2[2:4] + r43[1:3]).astype(BF), 1)
    r2, r1, wa, wc = lax.optimization_barrier((r2, r1, along_y(wa), over_y(wc, 2)))
    for_me = s2[4] + r2[0].astype(F32) + r1[0].astype(F32)
    for_sibling = (r2[1].astype(F32) + r1[1].astype(F32)).astype(BF)
    second, h23 = lax.optimization_barrier((over_core(for_sibling), h23))
    total = totals(offset, own_grad, for_me, second)
    total = total.reshape(seg_dev * seg_len, 2 * HD)

    crossed = over_xlo(total)
    from_y = [total, over_y(total, 1), None, over_y(total, 3)]
    crossed, from_y[1], from_y[3] = lax.optimization_barrier((crossed, from_y[1], from_y[3]))
    beside = over_core(total)
    group = [total, beside, crossed, over_core(crossed)]
    near_mine, near_other = close_part(h0, from_core, away, *group[:2])
    near_mine = near_mine + over_xlo(near_other).astype(F32)

    p43, p2 = far_part(h0, from_core, h23, group)
    p2, from_y[2] = lax.optimization_barrier((p2, over_y(total, 2)))
    p43 = along_z(p43, 2)
    p43 = p43.astype(F32)
    p2 = along_z(jnp.stack([p2[0] + p43[0], p2[1]]).astype(BF), 2)
    p1 = along_z((near_mine[0:2] + p43[1:3]).astype(BF), 1)
    mine, other, other2 = hidden_part([w0, wa, over_core(wa), wc, over_core(wc)], from_y)

    weight_sum = near_mine[2] + p2[0].astype(F32) + p1[0].astype(F32)
    weight_sibling = (p2[1].astype(F32) + p1[1].astype(F32)).astype(BF)
    weight_sibling, other, other2 = lax.optimization_barrier(
        (over_core(weight_sibling), over_xhi(other), over_xhi(other2))
    )
    weight_sum = weight_sum + weight_sibling.astype(F32)
    other = jnp.stack([other, other2]).astype(F32)
    hidden_grad = (mine.reshape(other.shape) + other).astype(BF)
    weight_grad = jnp.stack([weight_sum[:, :HD], weight_sum[:, HD:]])
    return (attended, query_grad, hidden_grad, weight_grad)


def solution(mesh):
    return jax.shard_map(
        local,
        mesh=mesh,
        in_specs=(
            P("dp", None, None),
            P(None, None, "mp"),
            P("dp", None, "mp"),
            P("dp", None, "mp"),
            P(),
            P(),
            P(),
        ),
        out_specs=(
            P("dp", None, "mp"),
            P("dp", None, "mp"),
            P("dp", None, "mp"),
            P(None, "dp", "mp"),
        ),
        check_vma=False,
    )
```

```python
import jax
import jax.numpy as jnp
from jax import lax
from jax.experimental import pallas as pl
from jax.experimental.pallas import tpu as pltpu
from jax.sharding import PartitionSpec as P

HD = 128
DEPTH = 4
NZ = 8
NY = 4
MASKED = -1e30
LOG2E = 1.4426950408889634
BF = jnp.bfloat16
F32 = jnp.float32
NT = (((1,), (1,)), ((), ()))


def over_core(x):
    return lax.ppermute(x, "dp", [(d, d ^ 1) for d in range(32)])


def over_xlo(x):
    return lax.ppermute(x, "dp", [(d, d ^ 2) for d in range(32)])


def along_z(x, steps):
    return lax.ppermute(
        x, "dp", [(d, (d + (4 * steps if d % 2 == 0 else -4 * steps)) % 32) for d in range(32)]
    )


def over_y(x, step):
    return lax.ppermute(x, "mp", [(m, (m & 4) | ((m + step) & 3)) for m in range(8)])


def along_y(x):
    pairs = []
    for d in range(32):
        for m in range(8):
            to = (m & 4) | ((m + (1 if d % 2 == 0 else -1)) & 3)
            pairs.append((d * 8 + m, d * 8 + to))
    return lax.ppermute(x, ("dp", "mp"), pairs)


def over_xhi(x):
    return lax.ppermute(x, "mp", [(m, m ^ 4) for m in range(8)])


def bits(x, low, count):
    return jnp.bitwise_and(lax.shift_right_logical(x, jnp.int32(low)), (1 << count) - 1)


def carrier(ahead, core):
    middle = jnp.bitwise_and(ahead, 3) == 0
    who = jnp.where(middle, core, lax.shift_right_logical(ahead, jnp.int32(2)))
    steps = jnp.where(ahead > 4, NZ - ahead, ahead)
    other = jnp.bitwise_xor(core, who)
    place = jnp.where(steps == 4, 0, jnp.where(steps == 0, 7, 7 - 2 * steps + other))
    return who, place


def smem():
    return pl.BlockSpec(memory_space=pltpu.SMEM)


def vmem():
    return pl.BlockSpec(memory_space=pltpu.VMEM)


def cost(us):
    return pl.CostEstimate(flops=int(us * 1.1e9) if us > 6 else 1 << 10, bytes_accessed=1 << 10, transcendentals=0)


def project_kernel(
    parents, placement, hidden, weight,
    own, sent, pair, offset, tiles, w0, wa, wc, h_sem, w_sem, wb, wd, ups, places, i_sem,
):
    lists = [
        pltpu.make_async_copy(parents, ups, i_sem.at[0]),
        pltpu.make_async_copy(placement, places, i_sem.at[1]),
    ]
    for copy in lists:
        copy.start()
    y = bits(lax.axis_index("mp"), 0, 2)
    rows, tile = tiles.shape[1], tiles.shape[2]
    copies = []
    core = bits(lax.axis_index("dp"), 0, 1)
    near = jnp.where(core == 0, 1, NY - 1)
    for step, steps in enumerate((0, near, 2, NY - near)):
        for x in range(2):
            k = 2 * step + x
            at = x * NY + jnp.bitwise_and(y + steps, NY - 1)
            part = pl.ds(pl.multiple_of(at * tile, 128), tile)
            h = pltpu.make_async_copy(hidden.at[:, part], tiles.at[at], h_sem.at[k])
            if step == 2:
                first = pltpu.make_async_copy(weight.at[core, part], wc.at[x], w_sem.at[k])
                last = pltpu.make_async_copy(weight.at[1 - core, part], wd.at[x], w_sem.at[8 + x])
                w = (first, last)
            else:
                out = {0: w0, 1: wa, 3: wb}[step]
                w = (pltpu.make_async_copy(weight.at[:, part], out.at[:, x], w_sem.at[k]),)
            for copy in (h, *w):
                copy.start()
            copies.append((h, w, at, step, x))
    for copy in lists:
        copy.wait()
    slot = lax.axis_index("dp") * 2 + 1
    found = jnp.int32(0)
    for g in range(parents.shape[0]):
        up = ups[g]
        hit = (up >= 0) & (places[jnp.maximum(up, 0)] == slot)
        found = jnp.where(hit, 1, found)
    offset[0] = found
    total = None
    for h, w, at, step, x in copies:
        for copy in (h, *w):
            copy.wait()
        if step == 2:
            flip = core == 1
            first, last = wc[x], wd[x]
            both = jnp.concatenate([jnp.where(flip, last, first), jnp.where(flip, first, last)], axis=1)
        else:
            out = {0: w0, 1: wa, 3: wb}[step]
            both = jnp.concatenate([out[0, x], out[1, x]], axis=1)
        term = jnp.dot(tiles[at], both, preferred_element_type=F32)
        total = term if total is None else total + term
    key = total[:, :HD]
    high = key.astype(BF)
    rest = (key - high.astype(F32)).astype(BF)
    packed = jnp.concatenate([high, rest, total[:, HD:].astype(BF)], axis=1)
    own[0] = packed[: rows // 2]
    own[1] = packed[rows // 2 :]
    block = own[found]
    sent[...] = block
    pair[0] = block
    pair[1] = block


def project(parents, placement, hidden, weight):
    rows, width = hidden.shape
    count = 8
    hbm = pl.BlockSpec(memory_space=pltpu.HBM)
    return pl.pallas_call(
        project_kernel,
        in_specs=[hbm] * 4,
        out_specs=[vmem()] * 3 + [smem()] + [vmem()] * 4,
        out_shape=[
            pltpu.VMEM((2, rows // 2, 3 * HD), BF),
            pltpu.VMEM((rows // 2, 3 * HD), BF),
            pltpu.VMEM((2, rows // 2, 3 * HD), BF),
            jax.ShapeDtypeStruct((1,), jnp.int32),
            pltpu.VMEM((count, rows, width // count), BF),
        ]
        + [pltpu.VMEM((2, 2, width // count, HD), BF)] * 2
        + [pltpu.VMEM((2, width // count, HD), BF)],
        scratch_shapes=[
            pltpu.SemaphoreType.DMA((count,)),
            pltpu.SemaphoreType.DMA((count + 2,)),
            pltpu.VMEM((2, 2, width // count, HD), BF),
            pltpu.VMEM((2, width // count, HD), BF),
            pltpu.SMEM(parents.shape, jnp.int32),
            pltpu.SMEM(parents.shape, jnp.int32),
            pltpu.SemaphoreType.DMA((2,)),
        ],
        compiler_params=pltpu.CompilerParams(vmem_limit_bytes=8 << 20),
        cost_estimate=cost(5),
        name="project",
    )(*(pltpu.with_memory_space_constraint(v, pltpu.HBM) for v in (parents, placement, hidden, weight)))


def turn_kernel(tiles, here, to_xlo, away, to_core, turned):
    device = lax.axis_index("dp")
    zed, xlo, core = bits(device, 2, 3), bits(device, 1, 1), bits(device, 0, 1)
    chunk = here.shape[1]
    for tile in range(NZ):
        turned[tile] = tiles[tile].T.reshape(4, chunk, tiles.shape[1])
    early = to_xlo.shape[1]
    for d_core, d_xlo, out in ((1, 0, to_core.at[0]), (1, 1, to_core.at[1]), (0, 1, to_xlo.at[0]), (0, 0, here)):
        who = jnp.bitwise_xor(core, d_core)
        x = jnp.bitwise_xor(xlo, d_xlo)
        for place in range(NZ):
            steps = (4, 3, 3, 2, 2, 1, 1, 0)[place]
            other = (0, 0, 1, 0, 1, 0, 1, 0)[place]
            tile = jnp.bitwise_and(zed + jnp.where(who == 0, steps, NZ - steps), NZ - 1)
            piece = turned[tile, 2 * x + jnp.bitwise_xor(who, other)]
            if (d_core, d_xlo) == (0, 1) and place >= early:
                away[place - early] = piece
            else:
                out[place] = piece


def turn(tiles):
    count, rows, wide = tiles.shape
    chunk = wide // 4
    return pl.pallas_call(
        turn_kernel,
        in_specs=[vmem()],
        out_specs=[vmem()] * 4,
        out_shape=[
            pltpu.VMEM((NZ, chunk, rows), BF),
            pltpu.VMEM((2, 3, chunk, rows), BF),
            pltpu.VMEM((5, chunk, rows), BF),
            pltpu.VMEM((2, NZ, chunk, rows), BF),
        ],
        scratch_shapes=[pltpu.VMEM((count, 4, chunk, rows), BF)],
        compiler_params=pltpu.CompilerParams(vmem_limit_bytes=12 << 20),
        cost_estimate=cost(3),
        name="turn",
    )(tiles)


def attend_kernel(*refs):
    parents, placement, lengths, queries, grads, own = refs[:6]
    blocks = refs[6:26]
    probs_out, score_out, turned_out, own_grad, kept, sent = refs[26:32]
    key_rows, value_rows, bias, key_sum, value_sum, total, found = refs[32:]
    device = lax.axis_index("dp")
    zed, xlo, core = bits(device, 2, 3), bits(device, 1, 1), bits(device, 0, 1)
    count = parents.shape[0]
    length = queries.shape[1]
    scale = HD ** (-0.5)
    for i in range(2):
        slot = device * 2 + i
        segment = jnp.int32(0)
        for g in range(count):
            segment = jnp.where(placement[g] == slot, g, segment)
        found[8 * i] = lengths[segment]
        key_rows[4 * i] = own[i, :, : 2 * HD]
        value_rows[4 * i] = own[i, :, 2 * HD :]
        for j in range(1, DEPTH):
            up = jnp.where(segment >= 0, parents[jnp.maximum(segment, 0)], -1)
            there = up >= 0
            upper = jnp.maximum(up, 0)
            holder = jnp.where(there, bits(placement[upper], 1, 5), device)
            found[8 * i + j] = jnp.where(there, lengths[upper], 0)
            h_zed, h_core = bits(holder, 2, 3), bits(holder, 0, 1)
            d_xlo = jnp.bitwise_xor(bits(holder, 1, 1), xlo)
            who, place = carrier(jnp.bitwise_and(h_zed - zed, NZ - 1), h_core)
            found[8 * i + 4 + j] = jnp.where(who == core, 0, 16) + d_xlo * NZ + place
            who, place = carrier(jnp.bitwise_and(zed - h_zed, NZ - 1), h_core)
            found[16 + 4 * i + j] = jnp.where(who == core, 0, 16) + d_xlo * NZ + place
            segment = up

    def fetch(n, _):
        member = 4 * (n // 3) + n % 3 + 1
        at = found[16 + member]
        spot = jnp.bitwise_and(at, NZ - 1)
        for side in range(4):

            @pl.when(lax.shift_right_logical(at, jnp.int32(3)) == side)
            def _():
                for k, (first, many) in enumerate(((0, 1), (1, 2), (3, 2), (5, 2), (7, 1))):

                    @pl.when((spot >= first) & (spot < first + many))
                    def _():
                        ref = blocks[5 * side + k]
                        key_rows[member] = ref[spot - first, :, : 2 * HD]
                        value_rows[member] = ref[spot - first, :, 2 * HD :]

        return 0

    lax.fori_loop(0, 6, fetch, 0)
    total[...] = jnp.zeros_like(total)
    row = lax.broadcasted_iota(jnp.int32, (length, length), 0)
    col = lax.broadcasted_iota(jnp.int32, (length, length), 1)
    for i in range(2):
        own_len = found[8 * i]
        keys = key_rows[4 * i : 4 * i + 4].reshape(DEPTH * length, 2 * HD)
        values = value_rows[4 * i : 4 * i + 4].reshape(DEPTH * length, HD)
        bias[0:length] = jnp.where((row < own_len) & (row <= col), 0.0, MASKED)
        for j in range(1, DEPTH):
            bias[j * length : (j + 1) * length] = jnp.where(row < found[8 * i + j], 0.0, MASKED)
        turned_out[i, 0] = keys[:, :HD].T
        turned_out[i, 1] = values.T
        valid = lax.broadcasted_iota(jnp.int32, (1, 2 * length), 1)
        valid = jnp.bitwise_and(valid, length - 1) < own_len
        pairs = queries.shape[2] // HD // 2
        for pair in range(pairs):
            lo, mid, hi = 2 * pair * HD, (2 * pair + 1) * HD, (2 * pair + 2) * HD
            q2 = jnp.concatenate([queries[i, :, lo:mid], queries[i, :, mid:hi]], axis=0)
            g2 = jnp.concatenate([grads[i, :, lo:mid], grads[i, :, mid:hi]], axis=0)
            scores = lax.dot_general(
                keys, jnp.concatenate([q2, q2], axis=1), NT, preferred_element_type=F32
            )
            both = bias[...]
            scores = scores + jnp.concatenate([both, both], axis=1)
            top = jnp.max(scores, axis=0, keepdims=True)
            weights = jnp.exp2((scores - top) * (scale * LOG2E))
            inverse = 1.0 / jnp.maximum(jnp.sum(weights, axis=0, keepdims=True), 1.0)
            probs = weights * jnp.where(valid, inverse, 0.0)
            probs_b = probs.astype(BF)
            dprobs = lax.dot_general(values, g2, NT, preferred_element_type=F32)
            delta = jnp.sum(probs * dprobs, axis=0, keepdims=True)
            score_grad = (probs * (dprobs - delta)).astype(BF)
            probs_out[i * pairs + pair] = probs_b
            score_out[i * pairs + pair] = score_grad
            dv = jnp.dot(probs_b, g2, preferred_element_type=F32)
            dk = jnp.dot(score_grad, q2, preferred_element_type=F32)
            if pair == 0:
                value_sum[...] = dv
                key_sum[...] = dk
            else:
                value_sum[...] += dv
                key_sum[...] += dk
        own_grad[i, :, :HD] = key_sum[0:length] * scale
        own_grad[i, :, HD:] = value_sum[0:length]
        for j in range(1, DEPTH):
            part = slice(j * length, (j + 1) * length)
            at = found[8 * i + 4 + j]
            total[at, :, :HD] += key_sum[part] * scale
            total[at, :, HD:] += value_sum[part]
    kept[...] = total[0:16].astype(BF)
    sent[...] = total[16:32].astype(BF)


def attend(parents, placement, lengths, queries, grads, own, blocks):
    _, length, cols = queries.shape
    pairs = cols // HD
    return pl.pallas_call(
        attend_kernel,
        in_specs=[smem()] * 3 + [vmem()] * 23,
        out_specs=[vmem()] * 6,
        out_shape=[
            pltpu.VMEM((pairs, DEPTH * length, 2 * length), BF),
            pltpu.VMEM((pairs, DEPTH * length, 2 * length), BF),
            pltpu.VMEM((2, 2, HD, DEPTH * length), BF),
            pltpu.VMEM((2, length, 2 * HD), F32),
        ]
        + [pltpu.VMEM((16, length, 2 * HD), BF)] * 2,
        scratch_shapes=[
            pltpu.VMEM((8, length, 2 * HD), BF),
            pltpu.VMEM((8, length, HD), BF),
            pltpu.VMEM((DEPTH * length, length), F32),
            pltpu.VMEM((DEPTH * length, HD), F32),
            pltpu.VMEM((DEPTH * length, HD), F32),
            pltpu.VMEM((32, length, 2 * HD), F32),
            pltpu.SMEM((24,), jnp.int32),
        ],
        compiler_params=pltpu.CompilerParams(vmem_limit_bytes=16 << 20),
        cost_estimate=cost(7),
        name="attend",
    )(parents, placement, lengths, queries, grads, own, *blocks)


def finish_kernel(probs, score_grad, turned, out, query_grad):
    scale = HD ** (-0.5)
    length = out.shape[1]
    pairs = out.shape[2] // HD // 2
    for i in range(2):
        for pair in range(pairs):
            lo, mid, hi = 2 * pair * HD, (2 * pair + 1) * HD, (2 * pair + 2) * HD
            result = jnp.dot(turned[i, 1], probs[i * pairs + pair], preferred_element_type=F32)
            dq = jnp.dot(turned[i, 0], score_grad[i * pairs + pair], preferred_element_type=F32) * scale
            out[i, :, lo:mid] = result[:, :length].T.astype(BF)
            out[i, :, mid:hi] = result[:, length:].T.astype(BF)
            query_grad[i, :, lo:mid] = dq[:, :length].T.astype(BF)
            query_grad[i, :, mid:hi] = dq[:, length:].T.astype(BF)


def finish(probs, score_grad, turned, shape):
    return pl.pallas_call(
        finish_kernel,
        in_specs=[vmem()] * 3,
        out_specs=[vmem()] * 2,
        out_shape=[jax.ShapeDtypeStruct(shape, BF)] * 2,
        compiler_params=pltpu.CompilerParams(vmem_limit_bytes=24 << 20),
        cost_estimate=cost(2),
        name="finish",
    )(probs, score_grad, turned)


def total_kernel(offset, own, first, second, out):
    back = first[...] + second[...].astype(F32)
    for i in range(2):
        out[i] = (own[i] + jnp.where(offset[0] == i, back, 0.0)).astype(BF)


def totals(offset, own, first, second):
    return pl.pallas_call(
        total_kernel,
        in_specs=[smem(), vmem(), vmem(), vmem()],
        out_specs=vmem(),
        out_shape=pltpu.VMEM(own.shape, BF),
        compiler_params=pltpu.CompilerParams(vmem_limit_bytes=8 << 20),
        name="totals",
    )(offset, own, first, second)


def far_kernel(here, came, crossed, t0, t1, t2, t3, p43):
    chunk, rows = here.shape[1:]
    many = crossed.shape[1]
    part = None
    for h, t in ((here, t0), (came.at[0], t1), (crossed.at[0], t2), (crossed.at[1], t3)):
        left = h[:many].reshape(many * chunk, rows)
        term = jnp.dot(left, t[...], preferred_element_type=F32)
        part = term if part is None else part + term
    p43[...] = part.reshape(p43.shape).astype(BF)


def far_part(here, came, crossed, tot):
    chunk = here.shape[1]
    cols = tot[0].shape[1]
    return pl.pallas_call(
        far_kernel,
        in_specs=[vmem()] * 7,
        out_specs=vmem(),
        out_shape=pltpu.VMEM((crossed.shape[1], chunk, cols), BF),
        compiler_params=pltpu.CompilerParams(vmem_limit_bytes=12 << 20),
        cost_estimate=cost(1),
        name="far_part",
    )(here, came, crossed, *tot)


def close_kernel(here, came, away, t0, t1, mine, other):
    many, chunk, rows = away.shape
    first = here.shape[0] - many
    for ref, own, sibling in (
        (other, away[...], came[1, first:]),
        (mine, here[first:], came[0, first:]),
    ):
        part = jnp.dot(own.reshape(many * chunk, rows), t0[...], preferred_element_type=F32)
        part += jnp.dot(sibling.reshape(many * chunk, rows), t1[...], preferred_element_type=F32)
        ref[...] = part.reshape(ref.shape).astype(ref.dtype)


def close_part(here, came, away, t0, t1):
    shape = (*away.shape[:2], t0.shape[1])
    return pl.pallas_call(
        close_kernel,
        in_specs=[vmem()] * 5,
        out_specs=[vmem()] * 2,
        out_shape=[pltpu.VMEM(shape, F32), pltpu.VMEM(shape, BF)],
        compiler_params=pltpu.CompilerParams(vmem_limit_bytes=12 << 20),
        cost_estimate=cost(1),
        name="close_part",
    )(here, came, away, t0, t1)


def hidden_kernel(w0, wa, wb, wc, wd, t0, t1, t2, t3, mine, other, other2):
    xhi = bits(lax.axis_index("mp"), 2, 1)
    half = other.shape[0]
    for d in (1, 0):
        total = None
        at = jnp.bitwise_xor(xhi, d)
        flip = bits(lax.axis_index("dp"), 0, 1) == 1
        behind, ahead = t1[...], t3[...]
        pairs = (
            (w0[0, at], w0[1, at], t0[...]),
            (wa[0, at], wa[1, at], jnp.where(flip, ahead, behind)),
            (wb[0, at], wb[1, at], jnp.where(flip, behind, ahead)),
            (jnp.where(flip, wd[at], wc[at]), jnp.where(flip, wc[at], wd[at]), t2[...]),
        )
        for key, value, t in pairs:
            both = jnp.concatenate([key, value], axis=1)
            part = lax.dot_general(t, both, NT, preferred_element_type=F32)
            total = part if total is None else total + part
        if d:
            other[...] = total[:half].astype(BF)
            other2[...] = total[half:].astype(BF)
        else:
            mine[...] = total


def hidden_part(weights, tot):
    rows = tot[0].shape[0]
    cols = weights[0].shape[2]
    return pl.pallas_call(
        hidden_kernel,
        in_specs=[vmem()] * 9,
        out_specs=[vmem()] * 3,
        out_shape=[pltpu.VMEM((rows, cols), F32)] + [pltpu.VMEM((rows // 2, cols), BF)] * 2,
        compiler_params=pltpu.CompilerParams(vmem_limit_bytes=12 << 20),
        cost_estimate=cost(2),
        name="hidden_part",
    )(*weights, *tot)


def local(hidden, kv_weight, queries, out_grad, parents, placement, lengths):
    seg_dev, seg_len, width = hidden.shape
    flat = hidden.reshape(seg_dev * seg_len, width)

    own, block, pair, offset, tiles, w0, wa, wc = project(parents, placement, flat, kv_weight)

    x0 = over_xlo(block)
    pair = pair.at[1].set(over_core(block))
    z2, z1 = along_z(pair, 2), along_z(pair, 1)
    z3, z4 = along_z(z2, 1), along_z(z2[0], 2)

    h0, to_xlo, away, to_core = turn(tiles)
    from_core = over_core(to_core)
    to_xlo = to_xlo.at[1].set(from_core[1, :3])

    x1, x2 = over_xlo(z1), over_xlo(z2)
    z3, x1 = lax.optimization_barrier((z3, x1))
    z4, x2 = lax.optimization_barrier((z4, x2))
    x3, x4 = over_xlo(z3), over_xlo(z4)
    near = [z4[None], z3, z2, z1, block[None], x4[None], x3, x2, x1, x0[None]]
    far = [over_core(v) for v in near]

    probs, score_grad, member_t, own_grad, kept, sent = attend(
        parents, placement, lengths, queries, out_grad, own, near + far
    )

    came = over_core(sent)

    def both(first, last):
        return kept[first:last].astype(F32) + came[first:last].astype(F32)

    y1 = over_xlo(both(8, 11).astype(BF))
    y2 = over_xlo(both(11, 16).astype(BF))
    y1, to_xlo = lax.optimization_barrier((y1, to_xlo))
    h23 = over_xlo(to_xlo)
    r43 = along_z((both(0, 3) + y1.astype(F32)).astype(BF), 2).astype(F32)
    s2 = both(3, 8) + y2.astype(F32)
    r2 = along_z(jnp.stack([s2[0] + r43[0], s2[1]]).astype(BF), 2)
    r1 = along_z((s2[2:4] + r43[1:3]).astype(BF), 1)
    r2, r1 = lax.optimization_barrier((r2, r1))
    wa = along_y(wa)
    for_me = s2[4] + r2[0].astype(F32) + r1[0].astype(F32)
    for_sibling = (r2[1].astype(F32) + r1[1].astype(F32)).astype(BF)
    for_sibling, wa = lax.optimization_barrier((for_sibling, wa))
    second, h23 = lax.optimization_barrier((over_core(for_sibling), h23))
    total = totals(offset, own_grad, for_me, second)
    total = total.reshape(seg_dev * seg_len, 2 * HD)

    crossed = over_xlo(total)
    from_y = [total, over_y(total, 1), None, over_y(total, 3)]
    crossed, from_y[1], from_y[3], wc = lax.optimization_barrier(
        (crossed, from_y[1], from_y[3], over_y(wc, 2))
    )
    beside = over_core(total)
    group = [total, beside, crossed, over_core(crossed)]
    ours, crossed = lax.optimization_barrier((total, crossed))
    near_mine, near_other = close_part(h0, from_core, away, ours, beside)

    p43 = far_part(h0, from_core, h23, group)
    total, probs, p43 = lax.optimization_barrier((total, probs, p43))
    attended, query_grad = finish(probs, score_grad, member_t, queries.shape)
    near_other, from_y[2] = lax.optimization_barrier((over_xlo(near_other), over_y(total, 2)))
    near_mine = near_mine + near_other.astype(F32)
    mine, other, other2 = hidden_part([w0, wa, over_core(wa), wc, over_core(wc)], from_y)
    p43, attended, other, other2 = lax.optimization_barrier((along_z(p43, 2), attended, other, other2))
    p43 = p43.astype(F32)
    p2 = along_z(jnp.stack([near_mine[0] + p43[0], near_mine[1]]).astype(BF), 2)
    p1 = along_z((near_mine[2:4] + p43[1:3]).astype(BF), 1)
    p2, other, other2 = lax.optimization_barrier((p2, over_xhi(other), over_xhi(other2)))
    weight_sum = near_mine[4] + p2[0].astype(F32) + p1[0].astype(F32)
    weight_sibling = (p2[1].astype(F32) + p1[1].astype(F32)).astype(BF)
    weight_sum = weight_sum + over_core(weight_sibling).astype(F32)
    other = jnp.stack([other, other2]).astype(F32)
    hidden_grad = (mine.reshape(other.shape) + other).astype(BF)
    weight_grad = jnp.stack([weight_sum[:, :HD], weight_sum[:, HD:]])
    return (attended, query_grad, hidden_grad, weight_grad)


def solution(mesh):
    return jax.shard_map(
        local,
        mesh=mesh,
        in_specs=(
            P("dp", None, None),
            P(None, None, "mp"),
            P("dp", None, "mp"),
            P("dp", None, "mp"),
            P(),
            P(),
            P(),
        ),
        out_specs=(
            P("dp", None, "mp"),
            P("dp", None, "mp"),
            P("dp", None, "mp"),
            P(None, "dp", "mp"),
        ),
        check_vma=False,
    )
```

```python
import jax
import jax.numpy as jnp
from jax import lax
from jax.experimental import pallas as pl
from jax.experimental.pallas import tpu as pltpu
from jax.sharding import PartitionSpec as P

HD = 128
DEPTH = 4
NZ = 8
NY = 4
MASKED = -1e30
LOG2E = 1.4426950408889634
BF = jnp.bfloat16
F32 = jnp.float32
NT = (((1,), (1,)), ((), ()))


def over_core(x):
    return lax.ppermute(x, "dp", [(d, d ^ 1) for d in range(32)])


def over_xlo(x):
    return lax.ppermute(x, "dp", [(d, d ^ 2) for d in range(32)])


def along_z(x, steps):
    return lax.ppermute(
        x, "dp", [(d, (d + (4 * steps if d % 2 == 0 else -4 * steps)) % 32) for d in range(32)]
    )


def over_y(x, step):
    return lax.ppermute(x, "mp", [(m, (m & 4) | ((m + step) & 3)) for m in range(8)])


def along_y(x):
    pairs = []
    for d in range(32):
        for m in range(8):
            to = (m & 4) | ((m + (1 if d % 2 == 0 else -1)) & 3)
            pairs.append((d * 8 + m, d * 8 + to))
    return lax.ppermute(x, ("dp", "mp"), pairs)


def over_xhi(x):
    return lax.ppermute(x, "mp", [(m, m ^ 4) for m in range(8)])


def bits(x, low, count):
    return jnp.bitwise_and(lax.shift_right_logical(x, jnp.int32(low)), (1 << count) - 1)


def carrier(ahead, core):
    middle = jnp.bitwise_and(ahead, 3) == 0
    who = jnp.where(middle, core, lax.shift_right_logical(ahead, jnp.int32(2)))
    steps = jnp.where(ahead > 4, NZ - ahead, ahead)
    other = jnp.bitwise_xor(core, who)
    place = jnp.where(steps == 4, 0, jnp.where(steps == 0, 7, 7 - 2 * steps + other))
    return who, place


def smem():
    return pl.BlockSpec(memory_space=pltpu.SMEM)


def vmem():
    return pl.BlockSpec(memory_space=pltpu.VMEM)


def cost(us):
    return pl.CostEstimate(flops=int(us * 1.1e9) if us > 6 else 1 << 10, bytes_accessed=1 << 10, transcendentals=0)


def project_kernel(
    parents, placement, hidden, weight,
    own, sent, pair, offset, tiles, w0, wa, wc, h_sem, w_sem, wb, wd, ups, places, i_sem,
):
    lists = [
        pltpu.make_async_copy(parents, ups, i_sem.at[0]),
        pltpu.make_async_copy(placement, places, i_sem.at[1]),
    ]
    for copy in lists:
        copy.start()
    y = bits(lax.axis_index("mp"), 0, 2)
    rows, tile = tiles.shape[1], tiles.shape[2]
    copies = []
    core = bits(lax.axis_index("dp"), 0, 1)
    near = jnp.where(core == 0, 1, NY - 1)
    for step, steps in enumerate((0, near, 2, NY - near)):
        for x in range(2):
            k = 2 * step + x
            at = x * NY + jnp.bitwise_and(y + steps, NY - 1)
            part = pl.ds(pl.multiple_of(at * tile, 128), tile)
            h = pltpu.make_async_copy(hidden.at[:, part], tiles.at[at], h_sem.at[k])
            if step == 2:
                first = pltpu.make_async_copy(weight.at[core, part], wc.at[x], w_sem.at[k])
                last = pltpu.make_async_copy(weight.at[1 - core, part], wd.at[x], w_sem.at[8 + x])
                w = (first, last)
            else:
                out = {0: w0, 1: wa, 3: wb}[step]
                w = (pltpu.make_async_copy(weight.at[:, part], out.at[:, x], w_sem.at[k]),)
            for copy in (h, *w):
                copy.start()
            copies.append((h, w, at, step, x))
    for copy in lists:
        copy.wait()
    slot = lax.axis_index("dp") * 2 + 1
    found = jnp.int32(0)
    for g in range(parents.shape[0]):
        up = ups[g]
        hit = (up >= 0) & (places[jnp.maximum(up, 0)] == slot)
        found = jnp.where(hit, 1, found)
    offset[0] = found
    total = None
    for h, w, at, step, x in copies:
        for copy in (h, *w):
            copy.wait()
        if step == 2:
            flip = core == 1
            first, last = wc[x], wd[x]
            both = jnp.concatenate([jnp.where(flip, last, first), jnp.where(flip, first, last)], axis=1)
        else:
            out = {0: w0, 1: wa, 3: wb}[step]
            both = jnp.concatenate([out[0, x], out[1, x]], axis=1)
        term = jnp.dot(tiles[at], both, preferred_element_type=F32)
        total = term if total is None else total + term
    key = total[:, :HD]
    high = key.astype(BF)
    rest = (key - high.astype(F32)).astype(BF)
    packed = jnp.concatenate([high, rest, total[:, HD:].astype(BF)], axis=1)
    own[0] = packed[: rows // 2]
    own[1] = packed[rows // 2 :]
    block = own[found]
    sent[...] = block
    pair[0] = block
    pair[1] = block


def project(parents, placement, hidden, weight):
    rows, width = hidden.shape
    count = 8
    hbm = pl.BlockSpec(memory_space=pltpu.HBM)
    return pl.pallas_call(
        project_kernel,
        in_specs=[hbm] * 4,
        out_specs=[vmem()] * 3 + [smem()] + [vmem()] * 4,
        out_shape=[
            pltpu.VMEM((2, rows // 2, 3 * HD), BF),
            pltpu.VMEM((rows // 2, 3 * HD), BF),
            pltpu.VMEM((2, rows // 2, 3 * HD), BF),
            jax.ShapeDtypeStruct((1,), jnp.int32),
            pltpu.VMEM((count, rows, width // count), BF),
        ]
        + [pltpu.VMEM((2, 2, width // count, HD), BF)] * 2
        + [pltpu.VMEM((2, width // count, HD), BF)],
        scratch_shapes=[
            pltpu.SemaphoreType.DMA((count,)),
            pltpu.SemaphoreType.DMA((count + 2,)),
            pltpu.VMEM((2, 2, width // count, HD), BF),
            pltpu.VMEM((2, width // count, HD), BF),
            pltpu.SMEM(parents.shape, jnp.int32),
            pltpu.SMEM(parents.shape, jnp.int32),
            pltpu.SemaphoreType.DMA((2,)),
        ],
        compiler_params=pltpu.CompilerParams(vmem_limit_bytes=8 << 20),
        cost_estimate=cost(5),
        name="project",
    )(*(pltpu.with_memory_space_constraint(v, pltpu.HBM) for v in (parents, placement, hidden, weight)))


def turn_kernel(tiles, here, to_xlo, away, to_core, turned):
    device = lax.axis_index("dp")
    zed, xlo, core = bits(device, 2, 3), bits(device, 1, 1), bits(device, 0, 1)
    chunk = here.shape[1]
    for tile in range(NZ):
        turned[tile] = tiles[tile].T.reshape(4, chunk, tiles.shape[1])
    early = to_xlo.shape[1]
    for d_core, d_xlo, out in ((1, 0, to_core.at[0]), (1, 1, to_core.at[1]), (0, 1, to_xlo.at[0]), (0, 0, here)):
        who = jnp.bitwise_xor(core, d_core)
        x = jnp.bitwise_xor(xlo, d_xlo)
        for place in range(NZ):
            steps = (4, 3, 3, 2, 2, 1, 1, 0)[place]
            other = (0, 0, 1, 0, 1, 0, 1, 0)[place]
            tile = jnp.bitwise_and(zed + jnp.where(who == 0, steps, NZ - steps), NZ - 1)
            piece = turned[tile, 2 * x + jnp.bitwise_xor(who, other)]
            if (d_core, d_xlo) == (0, 1) and place >= early:
                away[place - early] = piece
            else:
                out[place] = piece


def turn(tiles):
    count, rows, wide = tiles.shape
    chunk = wide // 4
    return pl.pallas_call(
        turn_kernel,
        in_specs=[vmem()],
        out_specs=[vmem()] * 4,
        out_shape=[
            pltpu.VMEM((NZ, chunk, rows), BF),
            pltpu.VMEM((2, 3, chunk, rows), BF),
            pltpu.VMEM((5, chunk, rows), BF),
            pltpu.VMEM((2, NZ, chunk, rows), BF),
        ],
        scratch_shapes=[pltpu.VMEM((count, 4, chunk, rows), BF)],
        compiler_params=pltpu.CompilerParams(vmem_limit_bytes=12 << 20),
        cost_estimate=cost(3),
        name="turn",
    )(tiles)


def attend_kernel(*refs):
    parents, placement, lengths, queries, grads, own = refs[:6]
    blocks = refs[6:26]
    probs_out, score_out, turned_out, own_grad, kept, sent = refs[26:32]
    key_rows, value_rows, bias, key_sum, value_sum, total, found = refs[32:]
    device = lax.axis_index("dp")
    zed, xlo, core = bits(device, 2, 3), bits(device, 1, 1), bits(device, 0, 1)
    count = parents.shape[0]
    length = queries.shape[1]
    scale = HD ** (-0.5)
    for i in range(2):
        slot = device * 2 + i
        segment = jnp.int32(0)
        for g in range(count):
            segment = jnp.where(placement[g] == slot, g, segment)
        found[8 * i] = lengths[segment]
        key_rows[4 * i] = own[i, :, : 2 * HD]
        value_rows[4 * i] = own[i, :, 2 * HD :]
        for j in range(1, DEPTH):
            up = jnp.where(segment >= 0, parents[jnp.maximum(segment, 0)], -1)
            there = up >= 0
            upper = jnp.maximum(up, 0)
            holder = jnp.where(there, bits(placement[upper], 1, 5), device)
            found[8 * i + j] = jnp.where(there, lengths[upper], 0)
            h_zed, h_core = bits(holder, 2, 3), bits(holder, 0, 1)
            d_xlo = jnp.bitwise_xor(bits(holder, 1, 1), xlo)
            who, place = carrier(jnp.bitwise_and(h_zed - zed, NZ - 1), h_core)
            found[8 * i + 4 + j] = jnp.where(who == core, 0, 16) + d_xlo * NZ + place
            who, place = carrier(jnp.bitwise_and(zed - h_zed, NZ - 1), h_core)
            found[16 + 4 * i + j] = jnp.where(who == core, 0, 16) + d_xlo * NZ + place
            segment = up

    def fetch(n, _):
        member = 4 * (n // 3) + n % 3 + 1
        at = found[16 + member]
        spot = jnp.bitwise_and(at, NZ - 1)
        for side in range(4):

            @pl.when(lax.shift_right_logical(at, jnp.int32(3)) == side)
            def _():
                for k, (first, many) in enumerate(((0, 1), (1, 2), (3, 2), (5, 2), (7, 1))):

                    @pl.when((spot >= first) & (spot < first + many))
                    def _():
                        ref = blocks[5 * side + k]
                        key_rows[member] = ref[spot - first, :, : 2 * HD]
                        value_rows[member] = ref[spot - first, :, 2 * HD :]

        return 0

    lax.fori_loop(0, 6, fetch, 0)
    total[...] = jnp.zeros_like(total)
    row = lax.broadcasted_iota(jnp.int32, (length, length), 0)
    col = lax.broadcasted_iota(jnp.int32, (length, length), 1)
    for i in range(2):
        own_len = found[8 * i]
        keys = key_rows[4 * i : 4 * i + 4].reshape(DEPTH * length, 2 * HD)
        values = value_rows[4 * i : 4 * i + 4].reshape(DEPTH * length, HD)
        bias[0:length] = jnp.where((row < own_len) & (row <= col), 0.0, MASKED)
        for j in range(1, DEPTH):
            bias[j * length : (j + 1) * length] = jnp.where(row < found[8 * i + j], 0.0, MASKED)
        turned_out[i, 0] = keys[:, :HD].T
        turned_out[i, 1] = values.T
        pairs = queries.shape[2] // HD // 2
        heads = 8
        valid = lax.broadcasted_iota(jnp.int32, (1, heads * length), 1)
        valid = jnp.bitwise_and(valid, length - 1) < own_len
        for step in range(2 * pairs // heads):
            lanes = [slice((heads * step + n) * HD, (heads * step + n + 1) * HD) for n in range(heads)]
            q4 = jnp.concatenate([queries[i, :, lane] for lane in lanes], axis=0)
            g4 = jnp.concatenate([grads[i, :, lane] for lane in lanes], axis=0)
            scores = lax.dot_general(
                keys, jnp.concatenate([q4, q4], axis=1), NT, preferred_element_type=F32
            )
            scores = scores + jnp.concatenate([bias[...]] * heads, axis=1)
            top = jnp.max(scores, axis=0, keepdims=True)
            weights = jnp.exp2((scores - top) * (scale * LOG2E))
            inverse = 1.0 / jnp.maximum(jnp.sum(weights, axis=0, keepdims=True), 1.0)
            probs = weights * jnp.where(valid, inverse, 0.0)
            probs_b = probs.astype(BF)
            dprobs = lax.dot_general(values, g4, NT, preferred_element_type=F32)
            product = probs * dprobs
            delta = jnp.sum(product, axis=0, keepdims=True)
            score_grad = (product - probs * delta).astype(BF)
            for n in range(heads // 2):
                at = i * pairs + step * (heads // 2) + n
                probs_out[at] = probs_b[:, 2 * n * length : (2 * n + 2) * length]
                score_out[at] = score_grad[:, 2 * n * length : (2 * n + 2) * length]
            dv = jnp.dot(probs_b, g4, preferred_element_type=F32)
            dk = jnp.dot(score_grad, q4, preferred_element_type=F32)
            if step == 0:
                value_sum[...] = dv
                key_sum[...] = dk
            else:
                value_sum[...] += dv
                key_sum[...] += dk
        own_grad[i, :, :HD] = key_sum[0:length] * scale
        own_grad[i, :, HD:] = value_sum[0:length]
        for j in range(1, DEPTH):
            part = slice(j * length, (j + 1) * length)
            at = found[8 * i + 4 + j]
            total[at, :, :HD] += key_sum[part] * scale
            total[at, :, HD:] += value_sum[part]
    kept[...] = total[0:16].astype(BF)
    sent[...] = total[16:32].astype(BF)


def attend(parents, placement, lengths, queries, grads, own, blocks):
    _, length, cols = queries.shape
    pairs = cols // HD
    return pl.pallas_call(
        attend_kernel,
        in_specs=[smem()] * 3 + [vmem()] * 23,
        out_specs=[vmem()] * 6,
        out_shape=[
            pltpu.VMEM((pairs, DEPTH * length, 2 * length), BF),
            pltpu.VMEM((pairs, DEPTH * length, 2 * length), BF),
            pltpu.VMEM((2, 2, HD, DEPTH * length), BF),
            pltpu.VMEM((2, length, 2 * HD), F32),
        ]
        + [pltpu.VMEM((16, length, 2 * HD), BF)] * 2,
        scratch_shapes=[
            pltpu.VMEM((8, length, 2 * HD), BF),
            pltpu.VMEM((8, length, HD), BF),
            pltpu.VMEM((DEPTH * length, length), F32),
            pltpu.VMEM((DEPTH * length, HD), F32),
            pltpu.VMEM((DEPTH * length, HD), F32),
            pltpu.VMEM((32, length, 2 * HD), F32),
            pltpu.SMEM((24,), jnp.int32),
        ],
        compiler_params=pltpu.CompilerParams(vmem_limit_bytes=24 << 20),
        cost_estimate=cost(7),
        name="attend",
    )(parents, placement, lengths, queries, grads, own, *blocks)


def finish_kernel(probs, score_grad, turned, out, query_grad):
    scale = HD ** (-0.5)
    length = out.shape[1]
    pairs = out.shape[2] // HD // 2
    for i in range(2):
        for pair in range(pairs):
            lo, mid, hi = 2 * pair * HD, (2 * pair + 1) * HD, (2 * pair + 2) * HD
            result = jnp.dot(turned[i, 1], probs[i * pairs + pair], preferred_element_type=F32)
            dq = jnp.dot(turned[i, 0], score_grad[i * pairs + pair], preferred_element_type=F32) * scale
            out[i, :, lo:mid] = result[:, :length].T.astype(BF)
            out[i, :, mid:hi] = result[:, length:].T.astype(BF)
            query_grad[i, :, lo:mid] = dq[:, :length].T.astype(BF)
            query_grad[i, :, mid:hi] = dq[:, length:].T.astype(BF)


def finish(probs, score_grad, turned, shape):
    return pl.pallas_call(
        finish_kernel,
        in_specs=[vmem()] * 3,
        out_specs=[vmem()] * 2,
        out_shape=[jax.ShapeDtypeStruct(shape, BF)] * 2,
        compiler_params=pltpu.CompilerParams(vmem_limit_bytes=24 << 20),
        cost_estimate=cost(2),
        name="finish",
    )(probs, score_grad, turned)


def total_kernel(offset, own, first, second, out):
    back = first[...] + second[...].astype(F32)
    for i in range(2):
        out[i] = (own[i] + jnp.where(offset[0] == i, back, 0.0)).astype(BF)


def totals(offset, own, first, second):
    return pl.pallas_call(
        total_kernel,
        in_specs=[smem(), vmem(), vmem(), vmem()],
        out_specs=vmem(),
        out_shape=pltpu.VMEM(own.shape, BF),
        compiler_params=pltpu.CompilerParams(vmem_limit_bytes=8 << 20),
        name="totals",
    )(offset, own, first, second)


def far_kernel(here, came, crossed, t0, t1, t2, t3, p43):
    chunk, rows = here.shape[1:]
    many = crossed.shape[1]
    part = None
    for h, t in ((here, t0), (came.at[0], t1), (crossed.at[0], t2), (crossed.at[1], t3)):
        left = h[:many].reshape(many * chunk, rows)
        term = jnp.dot(left, t[...], preferred_element_type=F32)
        part = term if part is None else part + term
    p43[...] = part.reshape(p43.shape).astype(BF)


def far_part(here, came, crossed, tot):
    chunk = here.shape[1]
    cols = tot[0].shape[1]
    return pl.pallas_call(
        far_kernel,
        in_specs=[vmem()] * 7,
        out_specs=vmem(),
        out_shape=pltpu.VMEM((crossed.shape[1], chunk, cols), BF),
        compiler_params=pltpu.CompilerParams(vmem_limit_bytes=12 << 20),
        cost_estimate=cost(1),
        name="far_part",
    )(here, came, crossed, *tot)


def close_kernel(here, came, away, t0, t1, mine, other):
    many, chunk, rows = away.shape
    first = here.shape[0] - many
    for ref, own, sibling in (
        (other, away[...], came[1, first:]),
        (mine, here[first:], came[0, first:]),
    ):
        part = jnp.dot(own.reshape(many * chunk, rows), t0[...], preferred_element_type=F32)
        part += jnp.dot(sibling.reshape(many * chunk, rows), t1[...], preferred_element_type=F32)
        ref[...] = part.reshape(ref.shape).astype(ref.dtype)


def close_part(here, came, away, t0, t1):
    shape = (*away.shape[:2], t0.shape[1])
    return pl.pallas_call(
        close_kernel,
        in_specs=[vmem()] * 5,
        out_specs=[vmem()] * 2,
        out_shape=[pltpu.VMEM(shape, F32), pltpu.VMEM(shape, BF)],
        compiler_params=pltpu.CompilerParams(vmem_limit_bytes=12 << 20),
        cost_estimate=cost(1),
        name="close_part",
    )(here, came, away, t0, t1)


def hidden_kernel(w0, wa, wb, wc, wd, t0, t1, t2, t3, mine, other, other2):
    xhi = bits(lax.axis_index("mp"), 2, 1)
    half = other.shape[0]
    for d in (1, 0):
        total = None
        at = jnp.bitwise_xor(xhi, d)
        flip = bits(lax.axis_index("dp"), 0, 1) == 1
        behind, ahead = t1[...], t3[...]
        pairs = (
            (w0[0, at], w0[1, at], t0[...]),
            (wa[0, at], wa[1, at], jnp.where(flip, ahead, behind)),
            (wb[0, at], wb[1, at], jnp.where(flip, behind, ahead)),
            (jnp.where(flip, wd[at], wc[at]), jnp.where(flip, wc[at], wd[at]), t2[...]),
        )
        for key, value, t in pairs:
            both = jnp.concatenate([key, value], axis=1)
            part = lax.dot_general(t, both, NT, preferred_element_type=F32)
            total = part if total is None else total + part
        if d:
            other[...] = total[:half].astype(BF)
            other2[...] = total[half:].astype(BF)
        else:
            mine[...] = total


def hidden_part(weights, tot):
    rows = tot[0].shape[0]
    cols = weights[0].shape[2]
    return pl.pallas_call(
        hidden_kernel,
        in_specs=[vmem()] * 9,
        out_specs=[vmem()] * 3,
        out_shape=[pltpu.VMEM((rows, cols), F32)] + [pltpu.VMEM((rows // 2, cols), BF)] * 2,
        compiler_params=pltpu.CompilerParams(vmem_limit_bytes=12 << 20),
        cost_estimate=cost(2),
        name="hidden_part",
    )(*weights, *tot)


def local(hidden, kv_weight, queries, out_grad, parents, placement, lengths):
    seg_dev, seg_len, width = hidden.shape
    flat = hidden.reshape(seg_dev * seg_len, width)

    own, block, pair, offset, tiles, w0, wa, wc = project(parents, placement, flat, kv_weight)

    x0 = over_xlo(block)
    pair = pair.at[1].set(over_core(block))
    z2, z1 = along_z(pair, 2), along_z(pair, 1)
    z3, z4 = along_z(z2, 1), along_z(z2[0], 2)

    h0, to_xlo, away, to_core = turn(tiles)
    from_core = over_core(to_core)
    to_xlo = to_xlo.at[1].set(from_core[1, :3])

    x1, x2 = over_xlo(z1), over_xlo(z2)
    z3, x1 = lax.optimization_barrier((z3, x1))
    z4, x2 = lax.optimization_barrier((z4, x2))
    x3, x4 = over_xlo(z3), over_xlo(z4)
    near = [z4[None], z3, z2, z1, block[None], x4[None], x3, x2, x1, x0[None]]
    far = [over_core(v) for v in near]

    probs, score_grad, member_t, own_grad, kept, sent = attend(
        parents, placement, lengths, queries, out_grad, own, near + far
    )

    came = over_core(sent)

    def both(first, last):
        return kept[first:last].astype(F32) + came[first:last].astype(F32)

    y1 = over_xlo(both(8, 11).astype(BF))
    y2 = over_xlo(both(11, 16).astype(BF))
    y1, to_xlo = lax.optimization_barrier((y1, to_xlo))
    h23 = over_xlo(to_xlo)
    r43 = along_z((both(0, 3) + y1.astype(F32)).astype(BF), 2).astype(F32)
    s2 = both(3, 8) + y2.astype(F32)
    r2 = along_z(jnp.stack([s2[0] + r43[0], s2[1]]).astype(BF), 2)
    r1 = along_z((s2[2:4] + r43[1:3]).astype(BF), 1)
    r2, r1 = lax.optimization_barrier((r2, r1))
    wa = along_y(wa)
    for_me = s2[4] + r2[0].astype(F32) + r1[0].astype(F32)
    for_sibling = (r2[1].astype(F32) + r1[1].astype(F32)).astype(BF)
    for_sibling, wa = lax.optimization_barrier((for_sibling, wa))
    second, h23 = lax.optimization_barrier((over_core(for_sibling), h23))
    total = totals(offset, own_grad, for_me, second)
    total = total.reshape(seg_dev * seg_len, 2 * HD)

    crossed = over_xlo(total)
    from_y = [total, over_y(total, 1), None, over_y(total, 3)]
    crossed, from_y[1], from_y[3], wc = lax.optimization_barrier(
        (crossed, from_y[1], from_y[3], over_y(wc, 2))
    )
    beside = over_core(total)
    group = [total, beside, crossed, over_core(crossed)]
    ours, crossed = lax.optimization_barrier((total, crossed))
    near_mine, near_other = close_part(h0, from_core, away, ours, beside)

    p43 = far_part(h0, from_core, h23, group)
    total, probs, p43 = lax.optimization_barrier((total, probs, p43))
    attended, query_grad = finish(probs, score_grad, member_t, queries.shape)
    near_other, from_y[2] = lax.optimization_barrier((over_xlo(near_other), over_y(total, 2)))
    near_mine = near_mine + near_other.astype(F32)
    mine, other, other2 = hidden_part([w0, wa, over_core(wa), wc, over_core(wc)], from_y)
    p43, attended, other, other2 = lax.optimization_barrier((along_z(p43, 2), attended, other, other2))
    p43 = p43.astype(F32)
    p2 = along_z(jnp.stack([near_mine[0] + p43[0], near_mine[1]]).astype(BF), 2)
    p1 = along_z((near_mine[2:4] + p43[1:3]).astype(BF), 1)
    p2, other, other2 = lax.optimization_barrier((p2, over_xhi(other), over_xhi(other2)))
    weight_sum = near_mine[4] + p2[0].astype(F32) + p1[0].astype(F32)
    weight_sibling = (p2[1].astype(F32) + p1[1].astype(F32)).astype(BF)
    weight_sum = weight_sum + over_core(weight_sibling).astype(F32)
    other = jnp.stack([other, other2]).astype(F32)
    hidden_grad = (mine.reshape(other.shape) + other).astype(BF)
    weight_grad = jnp.stack([weight_sum[:, :HD], weight_sum[:, HD:]])
    return (attended, query_grad, hidden_grad, weight_grad)


def solution(mesh):
    return jax.shard_map(
        local,
        mesh=mesh,
        in_specs=(
            P("dp", None, None),
            P(None, None, "mp"),
            P("dp", None, "mp"),
            P("dp", None, "mp"),
            P(),
            P(),
            P(),
        ),
        out_specs=(
            P("dp", None, "mp"),
            P("dp", None, "mp"),
            P("dp", None, "mp"),
            P(None, "dp", "mp"),
        ),
        check_vma=False,
    )
```

```python
import jax
import jax.numpy as jnp
from jax import lax
from jax.experimental import pallas as pl
from jax.experimental.pallas import tpu as pltpu
from jax.sharding import PartitionSpec as P

HD = 128
DEPTH = 4
NZ = 8
NY = 4
MASKED = -1e30
LOG2E = 1.4426950408889634
BF = jnp.bfloat16
F32 = jnp.float32
NT = (((1,), (1,)), ((), ()))


def over_core(x):
    return lax.ppermute(x, "dp", [(d, d ^ 1) for d in range(32)])


def over_xlo(x):
    return lax.ppermute(x, "dp", [(d, d ^ 2) for d in range(32)])


def along_z(x, steps):
    return lax.ppermute(
        x, "dp", [(d, (d + (4 * steps if d % 2 == 0 else -4 * steps)) % 32) for d in range(32)]
    )


def over_y(x, step):
    return lax.ppermute(x, "mp", [(m, (m & 4) | ((m + step) & 3)) for m in range(8)])


def along_y(x):
    pairs = []
    for d in range(32):
        for m in range(8):
            to = (m & 4) | ((m + (1 if d % 2 == 0 else -1)) & 3)
            pairs.append((d * 8 + m, d * 8 + to))
    return lax.ppermute(x, ("dp", "mp"), pairs)


def over_xhi(x):
    return lax.ppermute(x, "mp", [(m, m ^ 4) for m in range(8)])


def bits(x, low, count):
    return jnp.bitwise_and(lax.shift_right_logical(x, jnp.int32(low)), (1 << count) - 1)


def carrier(ahead, core):
    middle = jnp.bitwise_and(ahead, 3) == 0
    who = jnp.where(middle, core, lax.shift_right_logical(ahead, jnp.int32(2)))
    steps = jnp.where(ahead > 4, NZ - ahead, ahead)
    other = jnp.bitwise_xor(core, who)
    place = jnp.where(steps == 4, 0, jnp.where(steps == 0, 7, 7 - 2 * steps + other))
    return who, place


def smem():
    return pl.BlockSpec(memory_space=pltpu.SMEM)


def vmem():
    return pl.BlockSpec(memory_space=pltpu.VMEM)


def cost(us):
    return pl.CostEstimate(flops=int(us * 1.1e9) if us > 6 else 1 << 10, bytes_accessed=1 << 10, transcendentals=0)


def project_kernel(
    parents, placement, hidden, weight,
    own, sent, pair, offset, tiles, w0, wa, wc, h_sem, w_sem, wb, wd, ups, places, i_sem,
):
    lists = [
        pltpu.make_async_copy(parents, ups, i_sem.at[0]),
        pltpu.make_async_copy(placement, places, i_sem.at[1]),
    ]
    for copy in lists:
        copy.start()
    y = bits(lax.axis_index("mp"), 0, 2)
    rows, tile = tiles.shape[1], tiles.shape[2]
    copies = []
    core = bits(lax.axis_index("dp"), 0, 1)
    near = jnp.where(core == 0, 1, NY - 1)
    for step, steps in enumerate((0, near, 2, NY - near)):
        for x in range(2):
            k = 2 * step + x
            at = x * NY + jnp.bitwise_and(y + steps, NY - 1)
            part = pl.ds(pl.multiple_of(at * tile, 128), tile)
            h = pltpu.make_async_copy(hidden.at[:, part], tiles.at[at], h_sem.at[k])
            if step == 2:
                first = pltpu.make_async_copy(weight.at[core, part], wc.at[x], w_sem.at[k])
                last = pltpu.make_async_copy(weight.at[1 - core, part], wd.at[x], w_sem.at[8 + x])
                w = (first, last)
            else:
                out = {0: w0, 1: wa, 3: wb}[step]
                w = (pltpu.make_async_copy(weight.at[:, part], out.at[:, x], w_sem.at[k]),)
            for copy in (h, *w):
                copy.start()
            copies.append((h, w, at, step, x))
    for copy in lists:
        copy.wait()
    slot = lax.axis_index("dp") * 2 + 1
    found = jnp.int32(0)
    for g in range(parents.shape[0]):
        up = ups[g]
        hit = (up >= 0) & (places[jnp.maximum(up, 0)] == slot)
        found = jnp.where(hit, 1, found)
    offset[0] = found
    total = None
    for h, w, at, step, x in copies:
        for copy in (h, *w):
            copy.wait()
        if step == 2:
            flip = core == 1
            first, last = wc[x], wd[x]
            both = jnp.concatenate([jnp.where(flip, last, first), jnp.where(flip, first, last)], axis=1)
        else:
            out = {0: w0, 1: wa, 3: wb}[step]
            both = jnp.concatenate([out[0, x], out[1, x]], axis=1)
        term = jnp.dot(tiles[at], both, preferred_element_type=F32)
        total = term if total is None else total + term
    key = total[:, :HD]
    high = key.astype(BF)
    rest = (key - high.astype(F32)).astype(BF)
    packed = jnp.concatenate([high, rest, total[:, HD:].astype(BF)], axis=1)
    own[0] = packed[: rows // 2]
    own[1] = packed[rows // 2 :]
    block = own[found]
    sent[...] = block
    pair[0] = block
    pair[1] = block


def project(parents, placement, hidden, weight):
    rows, width = hidden.shape
    count = 8
    hbm = pl.BlockSpec(memory_space=pltpu.HBM)
    return pl.pallas_call(
        project_kernel,
        in_specs=[hbm] * 4,
        out_specs=[vmem()] * 3 + [smem()] + [vmem()] * 4,
        out_shape=[
            pltpu.VMEM((2, rows // 2, 3 * HD), BF),
            pltpu.VMEM((rows // 2, 3 * HD), BF),
            pltpu.VMEM((2, rows // 2, 3 * HD), BF),
            jax.ShapeDtypeStruct((1,), jnp.int32),
            pltpu.VMEM((count, rows, width // count), BF),
        ]
        + [pltpu.VMEM((2, 2, width // count, HD), BF)] * 2
        + [pltpu.VMEM((2, width // count, HD), BF)],
        scratch_shapes=[
            pltpu.SemaphoreType.DMA((count,)),
            pltpu.SemaphoreType.DMA((count + 2,)),
            pltpu.VMEM((2, 2, width // count, HD), BF),
            pltpu.VMEM((2, width // count, HD), BF),
            pltpu.SMEM(parents.shape, jnp.int32),
            pltpu.SMEM(parents.shape, jnp.int32),
            pltpu.SemaphoreType.DMA((2,)),
        ],
        compiler_params=pltpu.CompilerParams(vmem_limit_bytes=8 << 20),
        cost_estimate=cost(5),
        name="project",
    )(*(pltpu.with_memory_space_constraint(v, pltpu.HBM) for v in (parents, placement, hidden, weight)))


def turn_kernel(tiles, here, to_xlo, away, to_core, turned):
    device = lax.axis_index("dp")
    zed, xlo, core = bits(device, 2, 3), bits(device, 1, 1), bits(device, 0, 1)
    chunk = here.shape[1]
    for tile in range(NZ):
        turned[tile] = tiles[tile].T.reshape(4, chunk, tiles.shape[1])
    early = to_xlo.shape[1]
    for d_core, d_xlo, out in ((1, 0, to_core.at[0]), (1, 1, to_core.at[1]), (0, 1, to_xlo.at[0]), (0, 0, here)):
        who = jnp.bitwise_xor(core, d_core)
        x = jnp.bitwise_xor(xlo, d_xlo)
        for place in range(NZ):
            steps = (4, 3, 3, 2, 2, 1, 1, 0)[place]
            other = (0, 0, 1, 0, 1, 0, 1, 0)[place]
            tile = jnp.bitwise_and(zed + jnp.where(who == 0, steps, NZ - steps), NZ - 1)
            piece = turned[tile, 2 * x + jnp.bitwise_xor(who, other)]
            if (d_core, d_xlo) == (0, 1) and place >= early:
                away[place - early] = piece
            else:
                out[place] = piece


def turn(tiles):
    count, rows, wide = tiles.shape
    chunk = wide // 4
    return pl.pallas_call(
        turn_kernel,
        in_specs=[vmem()],
        out_specs=[vmem()] * 4,
        out_shape=[
            pltpu.VMEM((NZ, chunk, rows), BF),
            pltpu.VMEM((2, 3, chunk, rows), BF),
            pltpu.VMEM((5, chunk, rows), BF),
            pltpu.VMEM((2, NZ, chunk, rows), BF),
        ],
        scratch_shapes=[pltpu.VMEM((count, 4, chunk, rows), BF)],
        compiler_params=pltpu.CompilerParams(vmem_limit_bytes=12 << 20),
        cost_estimate=cost(3),
        name="turn",
    )(tiles)


def attend_kernel(*refs):
    parents, placement, lengths, queries, grads, own = refs[:6]
    blocks = refs[6:26]
    probs_out, score_out, turned_out, own_grad, kept, sent = refs[26:32]
    key_rows, value_rows, bias, total, found = refs[32:]
    device = lax.axis_index("dp")
    zed, xlo, core = bits(device, 2, 3), bits(device, 1, 1), bits(device, 0, 1)
    count = parents.shape[0]
    length = queries.shape[1]
    scale = HD ** (-0.5)
    for i in range(2):
        slot = device * 2 + i
        segment = jnp.int32(0)
        for g in range(count):
            segment = jnp.where(placement[g] == slot, g, segment)
        found[8 * i] = lengths[segment]
        key_rows[4 * i] = own[i, :, : 2 * HD]
        value_rows[4 * i] = own[i, :, 2 * HD :]
        for j in range(1, DEPTH):
            up = jnp.where(segment >= 0, parents[jnp.maximum(segment, 0)], -1)
            there = up >= 0
            upper = jnp.maximum(up, 0)
            holder = jnp.where(there, bits(placement[upper], 1, 5), device)
            found[8 * i + j] = jnp.where(there, lengths[upper], 0)
            h_zed, h_core = bits(holder, 2, 3), bits(holder, 0, 1)
            d_xlo = jnp.bitwise_xor(bits(holder, 1, 1), xlo)
            who, place = carrier(jnp.bitwise_and(h_zed - zed, NZ - 1), h_core)
            found[8 * i + 4 + j] = jnp.where(who == core, 0, 16) + d_xlo * NZ + place
            who, place = carrier(jnp.bitwise_and(zed - h_zed, NZ - 1), h_core)
            found[16 + 4 * i + j] = jnp.where(who == core, 0, 16) + d_xlo * NZ + place
            segment = up

    def fetch(n, _):
        member = 4 * (n // 3) + n % 3 + 1
        at = found[16 + member]
        spot = jnp.bitwise_and(at, NZ - 1)
        for side in range(4):

            @pl.when(lax.shift_right_logical(at, jnp.int32(3)) == side)
            def _():
                for k, (first, many) in enumerate(((0, 1), (1, 2), (3, 2), (5, 2), (7, 1))):

                    @pl.when((spot >= first) & (spot < first + many))
                    def _():
                        ref = blocks[5 * side + k]
                        key_rows[member] = ref[spot - first, :, : 2 * HD]
                        value_rows[member] = ref[spot - first, :, 2 * HD :]

        return 0

    lax.fori_loop(0, 6, fetch, 0)
    total[...] = jnp.zeros_like(total)
    row = lax.broadcasted_iota(jnp.int32, (length, length), 0)
    col = lax.broadcasted_iota(jnp.int32, (length, length), 1)
    for i in range(2):
        own_len = found[8 * i]
        keys = key_rows[4 * i : 4 * i + 4].reshape(DEPTH * length, 2 * HD)
        values = value_rows[4 * i : 4 * i + 4].reshape(DEPTH * length, HD)
        bias[0:length] = jnp.where((row < own_len) & (row <= col), 0.0, MASKED)
        for j in range(1, DEPTH):
            bias[j * length : (j + 1) * length] = jnp.where(row < found[8 * i + j], 0.0, MASKED)
        turned_out[i, 0] = keys[:, :HD].T
        turned_out[i, 1] = values.T
        pairs = queries.shape[2] // HD // 2
        heads = 8
        valid = lax.broadcasted_iota(jnp.int32, (1, heads * length), 1)
        valid = jnp.bitwise_and(valid, length - 1) < own_len
        for step in range(2 * pairs // heads):
            lanes = [slice((heads * step + n) * HD, (heads * step + n + 1) * HD) for n in range(heads)]
            q4 = jnp.concatenate([queries[i, :, lane] for lane in lanes], axis=0)
            g4 = jnp.concatenate([grads[i, :, lane] for lane in lanes], axis=0)
            scores = lax.dot_general(
                keys, jnp.concatenate([q4, q4], axis=1), NT, preferred_element_type=F32
            )
            scores = scores + jnp.concatenate([bias[...]] * heads, axis=1)
            top = jnp.max(scores, axis=0, keepdims=True)
            weights = jnp.exp2((scores - top) * (scale * LOG2E))
            inverse = 1.0 / jnp.maximum(jnp.sum(weights, axis=0, keepdims=True), 1.0)
            probs = weights * jnp.where(valid, inverse, 0.0)
            probs_b = probs.astype(BF)
            dprobs = lax.dot_general(values, g4, NT, preferred_element_type=F32)
            product = probs * dprobs
            delta = jnp.sum(product, axis=0, keepdims=True)
            score_grad = (product - probs * delta).astype(BF)
            for n in range(heads // 2):
                at = i * pairs + step * (heads // 2) + n
                probs_out[at] = probs_b[:, 2 * n * length : (2 * n + 2) * length]
                score_out[at] = score_grad[:, 2 * n * length : (2 * n + 2) * length]
            dv = jnp.dot(probs_b, g4, preferred_element_type=F32)
            dk = jnp.dot(score_grad, q4, preferred_element_type=F32)
            value_sum = dv if step == 0 else value_sum + dv
            key_sum = dk if step == 0 else key_sum + dk
        own_grad[i, :, :HD] = key_sum[0:length] * scale
        own_grad[i, :, HD:] = value_sum[0:length]
        for j in range(1, DEPTH):
            part = slice(j * length, (j + 1) * length)
            at = found[8 * i + 4 + j]
            total[at, :, :HD] += key_sum[part] * scale
            total[at, :, HD:] += value_sum[part]
    kept[...] = total[0:16].astype(BF)
    sent[...] = total[16:32].astype(BF)


def attend(parents, placement, lengths, queries, grads, own, blocks):
    _, length, cols = queries.shape
    pairs = cols // HD
    return pl.pallas_call(
        attend_kernel,
        in_specs=[smem()] * 3 + [vmem()] * 23,
        out_specs=[vmem()] * 6,
        out_shape=[
            pltpu.VMEM((pairs, DEPTH * length, 2 * length), BF),
            pltpu.VMEM((pairs, DEPTH * length, 2 * length), BF),
            pltpu.VMEM((2, 2, HD, DEPTH * length), BF),
            pltpu.VMEM((2, length, 2 * HD), F32),
        ]
        + [pltpu.VMEM((16, length, 2 * HD), BF)] * 2,
        scratch_shapes=[
            pltpu.VMEM((8, length, 2 * HD), BF),
            pltpu.VMEM((8, length, HD), BF),
            pltpu.VMEM((DEPTH * length, length), F32),
            pltpu.VMEM((32, length, 2 * HD), F32),
            pltpu.SMEM((24,), jnp.int32),
        ],
        compiler_params=pltpu.CompilerParams(vmem_limit_bytes=24 << 20),
        cost_estimate=cost(7),
        name="attend",
    )(parents, placement, lengths, queries, grads, own, *blocks)


def finish_kernel(probs, score_grad, turned, out, query_grad):
    scale = HD ** (-0.5)
    length = out.shape[1]
    pairs = out.shape[2] // HD // 2
    for i in range(2):
        for pair in range(pairs):
            lo, mid, hi = 2 * pair * HD, (2 * pair + 1) * HD, (2 * pair + 2) * HD
            result = jnp.dot(turned[i, 1], probs[i * pairs + pair], preferred_element_type=F32)
            dq = jnp.dot(turned[i, 0], score_grad[i * pairs + pair], preferred_element_type=F32) * scale
            out[i, :, lo:mid] = result[:, :length].T.astype(BF)
            out[i, :, mid:hi] = result[:, length:].T.astype(BF)
            query_grad[i, :, lo:mid] = dq[:, :length].T.astype(BF)
            query_grad[i, :, mid:hi] = dq[:, length:].T.astype(BF)


def finish(probs, score_grad, turned, shape):
    return pl.pallas_call(
        finish_kernel,
        in_specs=[vmem()] * 3,
        out_specs=[vmem()] * 2,
        out_shape=[jax.ShapeDtypeStruct(shape, BF)] * 2,
        compiler_params=pltpu.CompilerParams(vmem_limit_bytes=24 << 20),
        cost_estimate=cost(2),
        name="finish",
    )(probs, score_grad, turned)


def total_kernel(offset, own, first, second, out):
    back = first[...] + second[...].astype(F32)
    for i in range(2):
        out[i] = (own[i] + jnp.where(offset[0] == i, back, 0.0)).astype(BF)


def totals(offset, own, first, second):
    return pl.pallas_call(
        total_kernel,
        in_specs=[smem(), vmem(), vmem(), vmem()],
        out_specs=vmem(),
        out_shape=pltpu.VMEM(own.shape, BF),
        compiler_params=pltpu.CompilerParams(vmem_limit_bytes=8 << 20),
        name="totals",
    )(offset, own, first, second)


def far_kernel(here, came, crossed, t0, t1, t2, t3, p43):
    chunk, rows = here.shape[1:]
    many = crossed.shape[1]
    part = None
    for h, t in ((here, t0), (came.at[0], t1), (crossed.at[0], t2), (crossed.at[1], t3)):
        left = h[:many].reshape(many * chunk, rows)
        term = jnp.dot(left, t[...], preferred_element_type=F32)
        part = term if part is None else part + term
    p43[...] = part.reshape(p43.shape).astype(BF)


def far_part(here, came, crossed, tot):
    chunk = here.shape[1]
    cols = tot[0].shape[1]
    return pl.pallas_call(
        far_kernel,
        in_specs=[vmem()] * 7,
        out_specs=vmem(),
        out_shape=pltpu.VMEM((crossed.shape[1], chunk, cols), BF),
        compiler_params=pltpu.CompilerParams(vmem_limit_bytes=12 << 20),
        cost_estimate=cost(1),
        name="far_part",
    )(here, came, crossed, *tot)


def close_kernel(here, came, away, t0, t1, mine, other):
    many, chunk, rows = away.shape
    first = here.shape[0] - many
    for ref, own, sibling in (
        (other, away[...], came[1, first:]),
        (mine, here[first:], came[0, first:]),
    ):
        part = jnp.dot(own.reshape(many * chunk, rows), t0[...], preferred_element_type=F32)
        part += jnp.dot(sibling.reshape(many * chunk, rows), t1[...], preferred_element_type=F32)
        ref[...] = part.reshape(ref.shape).astype(ref.dtype)


def close_part(here, came, away, t0, t1):
    shape = (*away.shape[:2], t0.shape[1])
    return pl.pallas_call(
        close_kernel,
        in_specs=[vmem()] * 5,
        out_specs=[vmem()] * 2,
        out_shape=[pltpu.VMEM(shape, F32), pltpu.VMEM(shape, BF)],
        compiler_params=pltpu.CompilerParams(vmem_limit_bytes=12 << 20),
        cost_estimate=cost(1),
        name="close_part",
    )(here, came, away, t0, t1)


def hidden_kernel(w0, wa, wb, wc, wd, t0, t1, t2, t3, mine, other, other2):
    xhi = bits(lax.axis_index("mp"), 2, 1)
    half = other.shape[0]
    for d in (1, 0):
        total = None
        at = jnp.bitwise_xor(xhi, d)
        flip = bits(lax.axis_index("dp"), 0, 1) == 1
        behind, ahead = t1[...], t3[...]
        pairs = (
            (w0[0, at], w0[1, at], t0[...]),
            (wa[0, at], wa[1, at], jnp.where(flip, ahead, behind)),
            (wb[0, at], wb[1, at], jnp.where(flip, behind, ahead)),
            (jnp.where(flip, wd[at], wc[at]), jnp.where(flip, wc[at], wd[at]), t2[...]),
        )
        for key, value, t in pairs:
            both = jnp.concatenate([key, value], axis=1)
            part = lax.dot_general(t, both, NT, preferred_element_type=F32)
            total = part if total is None else total + part
        if d:
            other[...] = total[:half].astype(BF)
            other2[...] = total[half:].astype(BF)
        else:
            mine[...] = total


def hidden_part(weights, tot):
    rows = tot[0].shape[0]
    cols = weights[0].shape[2]
    return pl.pallas_call(
        hidden_kernel,
        in_specs=[vmem()] * 9,
        out_specs=[vmem()] * 3,
        out_shape=[pltpu.VMEM((rows, cols), F32)] + [pltpu.VMEM((rows // 2, cols), BF)] * 2,
        compiler_params=pltpu.CompilerParams(vmem_limit_bytes=12 << 20),
        cost_estimate=cost(2),
        name="hidden_part",
    )(*weights, *tot)


def local(hidden, kv_weight, queries, out_grad, parents, placement, lengths):
    seg_dev, seg_len, width = hidden.shape
    flat = hidden.reshape(seg_dev * seg_len, width)

    own, block, pair, offset, tiles, w0, wa, wc = project(parents, placement, flat, kv_weight)

    x0 = over_xlo(block)
    pair = pair.at[1].set(over_core(block))
    z2, z1 = along_z(pair, 2), along_z(pair, 1)
    z3, z4 = along_z(z2, 1), along_z(z2[0], 2)

    h0, to_xlo, away, to_core = turn(tiles)
    from_core = over_core(to_core)
    to_xlo = to_xlo.at[1].set(from_core[1, :3])

    x1, x2 = over_xlo(z1), over_xlo(z2)
    z3, x1 = lax.optimization_barrier((z3, x1))
    z4, x2 = lax.optimization_barrier((z4, x2))
    x3, x4 = over_xlo(z3), over_xlo(z4)
    near = [z4[None], z3, z2, z1, block[None], x4[None], x3, x2, x1, x0[None]]
    far = [over_core(v) for v in near]

    probs, score_grad, member_t, own_grad, kept, sent = attend(
        parents, placement, lengths, queries, out_grad, own, near + far
    )

    came = over_core(sent)

    def both(first, last):
        return kept[first:last].astype(F32) + came[first:last].astype(F32)

    y1 = over_xlo(both(8, 11).astype(BF))
    y2 = over_xlo(both(11, 16).astype(BF))
    y1, to_xlo = lax.optimization_barrier((y1, to_xlo))
    h23 = over_xlo(to_xlo)
    r43 = along_z((both(0, 3) + y1.astype(F32)).astype(BF), 2).astype(F32)
    s2 = both(3, 8) + y2.astype(F32)
    r2 = along_z(jnp.stack([s2[0] + r43[0], s2[1]]).astype(BF), 2)
    r1 = along_z((s2[2:4] + r43[1:3]).astype(BF), 1)
    r2, r1 = lax.optimization_barrier((r2, r1))
    wa = along_y(wa)
    for_me = s2[4] + r2[0].astype(F32) + r1[0].astype(F32)
    for_sibling = (r2[1].astype(F32) + r1[1].astype(F32)).astype(BF)
    for_sibling, wa = lax.optimization_barrier((for_sibling, wa))
    second, h23 = lax.optimization_barrier((over_core(for_sibling), h23))
    total = totals(offset, own_grad, for_me, second)
    total = total.reshape(seg_dev * seg_len, 2 * HD)

    crossed = over_xlo(total)
    from_y = [total, over_y(total, 1), None, over_y(total, 3)]
    crossed, from_y[1], from_y[3], wc = lax.optimization_barrier(
        (crossed, from_y[1], from_y[3], over_y(wc, 2))
    )
    beside = over_core(total)
    group = [total, beside, crossed, over_core(crossed)]
    ours, crossed = lax.optimization_barrier((total, crossed))
    near_mine, near_other = close_part(h0, from_core, away, ours, beside)

    p43 = far_part(h0, from_core, h23, group)
    total, probs, p43 = lax.optimization_barrier((total, probs, p43))
    attended, query_grad = finish(probs, score_grad, member_t, queries.shape)
    near_other, from_y[2] = lax.optimization_barrier((over_xlo(near_other), over_y(total, 2)))
    near_mine = near_mine + near_other.astype(F32)
    mine, other, other2 = hidden_part([w0, wa, over_core(wa), wc, over_core(wc)], from_y)
    p43, attended, other, other2 = lax.optimization_barrier((along_z(p43, 2), attended, other, other2))
    p43 = p43.astype(F32)
    p2 = along_z(jnp.stack([near_mine[0] + p43[0], near_mine[1]]).astype(BF), 2)
    p1 = along_z((near_mine[2:4] + p43[1:3]).astype(BF), 1)
    p2, other, other2 = lax.optimization_barrier((p2, over_xhi(other), over_xhi(other2)))
    weight_sum = near_mine[4] + p2[0].astype(F32) + p1[0].astype(F32)
    weight_sibling = (p2[1].astype(F32) + p1[1].astype(F32)).astype(BF)
    weight_sum = weight_sum + over_core(weight_sibling).astype(F32)
    other = jnp.stack([other, other2]).astype(F32)
    hidden_grad = (mine.reshape(other.shape) + other).astype(BF)
    weight_grad = jnp.stack([weight_sum[:, :HD], weight_sum[:, HD:]])
    return (attended, query_grad, hidden_grad, weight_grad)


def solution(mesh):
    return jax.shard_map(
        local,
        mesh=mesh,
        in_specs=(
            P("dp", None, None),
            P(None, None, "mp"),
            P("dp", None, "mp"),
            P("dp", None, "mp"),
            P(),
            P(),
            P(),
        ),
        out_specs=(
            P("dp", None, "mp"),
            P("dp", None, "mp"),
            P("dp", None, "mp"),
            P(None, "dp", "mp"),
        ),
        check_vma=False,
    )
```
